32 devices in a mesh: blk: 8 (over z, x), mp: 4 (over y, core).
Axes of the slice: x: 2, y: 2, z: 4, core: 2. Of those that a mesh axis runs over, the one named last changes fastest.
Arguments:
- hidden_in: bfloat16 [1024, 2048], P('blk'), may hold values from -6 to 6
- norm_gain: float32 [2048], replicated, may hold values from 0.25 to 1.75
- norm_bias: float32 [2048], replicated, may hold values from -3 to 3
- w_query: bfloat16 [2048, 2048], P(None, 'mp'), may hold values from -2 to 2
- w_key: bfloat16 [2048, 2048], P(None, 'mp'), may hold values from -0.125 to 0.125
- w_value: bfloat16 [2048, 2048], P(None, 'mp'), may hold values from -0.125 to 0.125
- w_out: bfloat16 [2048, 2048], P('mp'), may hold values from -0.125 to 0.125
- prefix_keys: bfloat16 [8, 128, 2048], P('blk', None, 'mp'), may hold values from -6 to 6
- prefix_values: bfloat16 [8, 128, 2048], P('blk', None, 'mp'), may hold values from -6 to 6
- segment: int32 [8, 128], P('blk'), may hold values from 0 to 3, never falling along the last dimension, each value on 1 to 64 neighbouring positions
- request_group: int32 [8, 4], P('blk'), may hold values from 0 to 3
- block_slot: int32 [8], P('blk'), may hold values from 0 to 7, each once
- block_live: int32 [8], P('blk'), may hold values 0 or 1
Outputs:
- hidden_out: bfloat16 [1024, 2048], P('blk')
The draws below stay inside these ranges and needn't reach their ends.
Inputs may be any that keep to these rules, and one draw needn't show every extreme that they name: Each row of segment counts requests 0 to 3 without falling; each request has 1 to 64 tokens. `block_slot`: each slot once.
All inputs are finite; a program needn't handle non-finite values. No bound on the sum of `block_live` on one device may be relied on, other than what follows from the above.
Results may differ from the reference program's by a relative error of at most 0.009.
Values may be sent and summed in bfloat16 or wider, within the bound.
No kernel may reach another device: no remote copies, remote signals or barrier semaphores. Data moves between devices by JAX's collectives and lax.ppermute only.
A program may use at most 128 MiB of HBM per device.

```python
import math
import jax
import jax.numpy as jnp
import numpy as np
from jax import lax

D = 2048
HEADS = 16
HD = 128
SUF_DEV = 128
REQ_DEV = 4
GROUPS = 4
BLOCK_TOK = 128
TOKENS = 1024
BLOCKS = 8


def draw_w_query(key, part):
    scale = 1.0 / jnp.sqrt(jnp.float32(D))
    base = jnp.clip(jax.random.normal(jax.random.fold_in(key, 11), (D, D), jnp.float32), -6.0, 6.0) * scale
    return base.astype(jnp.bfloat16)


def draw_prefix_keys(key, part):
    base = jnp.clip(jax.random.normal(jax.random.fold_in(key, 21), (BLOCKS, BLOCK_TOK, D), jnp.float32), -6.0, 6.0)
    return base.astype(jnp.bfloat16)


def with_ends(drawn, stream_key, least, top_value):
    longest = drawn.shape.index(max(drawn.shape))
    spots = []
    for shift in (0, 1):
        where = [jax.random.randint(jax.random.fold_in(stream_key, axis), (), 0, length) for axis, length in enumerate(drawn.shape)]
        where[longest] = (where[longest] + shift) % drawn.shape[longest]
        spots.append(tuple(where))
    return drawn.at[spots[0]].set(least).at[spots[1]].set(top_value)


def block_levels(stream_key, shape, cuts, smallest, top_value):
    level = 1.0
    for dim, blocks in cuts:
        draws = jax.random.uniform(jax.random.fold_in(jax.random.fold_in(stream_key, 6), dim), (blocks,), jnp.float32, smallest / len(cuts), top_value / len(cuts))
        level = level * jnp.repeat(jnp.exp(draws), shape[dim] // blocks).reshape((-1,) + (1,) * (len(shape) - 1 - dim))
    return level


def split_up(amount, total, reach, skew):
    loads = [(1 << 20) // math.isqrt(grade ** skew) + 1 for grade in range(2, amount + 1)]
    surplus, given = total - reach - (amount - 1), [1] * (amount - 1)
    while surplus > 0:
        free = [i for i in range(amount - 1) if given[i] < reach]
        whole, left = sum([loads[i] for i in free]), surplus
        for i in free:
            addition = min(reach - given[i], max(1, left * loads[i] // whole), surplus)
            given[i] = given[i] + addition
            surplus = surplus - addition
    return np.array([reach] + given)


def ragged(key, count, total, limit, slope):
    if count == 2:
        one = jax.random.randint(key, (), max(1, total - limit), min(limit, total - 1) + 1)
        return jnp.stack([one, total - one])
    tallies = jnp.asarray(split_up(count, total, limit, slope), jnp.int32)
    couples = (count - 1) // 2
    source_of, receiver = tallies[1:1 + 2 * couples:2], tallies[2:2 + 2 * couples:2]
    room = jnp.minimum(source_of - 1, limit - receiver)
    passed = jax.random.randint(jax.random.fold_in(key, 1), (couples,), 0, 1 << 20) % (room + 1)
    tallies = tallies.at[1:1 + 2 * couples:2].set(source_of - passed).at[2:2 + 2 * couples:2].set(receiver + passed)
    return tallies[jax.random.permutation(jax.random.fold_in(key, 2), count)]


def gaussian(own_key, shape, deviation, limit, pieces=(), kind=jnp.bfloat16):
    drawn = deviation * jax.random.normal(own_key, shape, jnp.float32)
    if pieces:
        drawn = drawn * block_levels(own_key, shape, pieces, -0.22, 0.18)
    return jnp.clip(drawn, -limit, limit).astype(kind)


def setup_inputs(seed: int = 0) -> dict:
    seeds = jax.random.split(jax.random.key(seed), 14)
    return {
        "hidden_in": gaussian(seeds[0], (TOKENS, D), 1.0, 6.0, ((0, 8),)),
        "norm_gain": jnp.clip(1.0 + 0.15 * jax.random.normal(seeds[1], (D,), jnp.float32), 0.25, 1.75),
        "norm_bias": gaussian(seeds[2], (D,), 0.5, 3.0, (), jnp.float32),
        "w_query": draw_w_query(jax.random.fold_in(seeds[13], 71), 0),
        "w_key": gaussian(seeds[4], (D, D), D ** -0.5, 0.125, ((1, 4),)),
        "w_value": gaussian(seeds[5], (D, D), D ** -0.5, 0.125, ((1, 4),)),
        "w_out": gaussian(seeds[6], (D, D), D ** -0.5, 0.125, ((0, 4),)),
        "prefix_keys": draw_prefix_keys(jax.random.fold_in(seeds[13], 71), 0),
        "prefix_values": gaussian(seeds[8], (BLOCKS, BLOCK_TOK, D), 1.0, 6.0, ((0, 8), (2, 4))),
        "segment": jax.vmap(lambda own: jnp.searchsorted(jnp.cumsum(ragged(own, REQ_DEV, SUF_DEV, SUF_DEV // 2, 2)), jnp.arange(SUF_DEV), side="right"))(jax.random.split(seeds[9], BLOCKS)).reshape((BLOCKS, SUF_DEV)).astype(jnp.int32),
        "request_group": with_ends(jax.random.randint(seeds[10], (BLOCKS, REQ_DEV), 0, GROUPS), jax.random.fold_in(seeds[10], 1), 0, GROUPS - 1).astype(jnp.int32),
        "block_slot": jax.random.permutation(seeds[11], BLOCKS).astype(jnp.int32),
        "block_live": with_ends((jax.random.randint(seeds[12], (BLOCKS,), 0, 4) < 3).astype(jnp.int32), jax.random.fold_in(seeds[12], 1), 0, 1),
    }


big = 1e+30

def layer_norm(values, gain, bias):
    mean = lax.optimization_barrier(jnp.mean(values, axis=-1, keepdims=True))
    centred = values - mean
    var = lax.optimization_barrier(jnp.mean(centred * centred, axis=-1, keepdims=True))
    return centred * lax.rsqrt(var + 1e-05) * gain + bias

def reference(hidden_in, norm_gain, norm_bias, w_query, w_key, w_value, w_out, prefix_keys, prefix_values, segment, request_group, block_slot, block_live):
    inputs = hidden_in.astype(jnp.float32)
    normed = layer_norm(inputs, norm_gain, norm_bias).astype(jnp.bfloat16)
    query = (jnp.dot(normed, w_query, preferred_element_type=jnp.float32) / jnp.sqrt(jnp.float32(HD))).astype(jnp.bfloat16)
    key = jnp.dot(normed, w_key, preferred_element_type=jnp.float32).astype(jnp.bfloat16)
    value = jnp.dot(normed, w_value, preferred_element_type=jnp.float32).astype(jnp.bfloat16)
    block_group = jnp.where(block_live == 1, block_slot * GROUPS // BLOCKS, -1)
    key_tags = jnp.repeat(block_group, BLOCK_TOK)
    all_keys = prefix_keys.reshape(BLOCKS * BLOCK_TOK, HEADS, HD).astype(jnp.float32)
    all_values = prefix_values.reshape(BLOCKS * BLOCK_TOK, HEADS, HD).astype(jnp.float32)
    places = jnp.arange(SUF_DEV)

    def one_row(row):
        start = (row * SUF_DEV).astype(jnp.int32)
        q_rows = lax.dynamic_slice_in_dim(query, start, SUF_DEV, 0).reshape(SUF_DEV, HEADS, HD).astype(jnp.float32)
        k_rows = lax.dynamic_slice_in_dim(key, start, SUF_DEV, 0).reshape(SUF_DEV, HEADS, HD).astype(jnp.float32)
        v_rows = lax.dynamic_slice_in_dim(value, start, SUF_DEV, 0).reshape(SUF_DEV, HEADS, HD).astype(jnp.float32)
        seg_row = segment[row]
        groups_row = request_group[row]
        token_group = lax.optimization_barrier(jnp.sum(jnp.where(seg_row[:, None] == jnp.arange(REQ_DEV)[None, :], groups_row[None, :], 0), axis=1))
        pre_scores = jnp.einsum('qhd,khd->hqk', q_rows, all_keys)
        pre_mask = token_group[:, None] == key_tags[None, :]
        loc_scores = jnp.einsum('qhd,khd->hqk', q_rows, k_rows)
        loc_mask = (seg_row[:, None] == seg_row[None, :]) & (places[None, :] <= places[:, None])
        scores = jnp.concatenate([pre_scores, loc_scores], axis=2)
        mask = jnp.concatenate([pre_mask, loc_mask], axis=1)[None]
        top = lax.optimization_barrier(jnp.max(jnp.where(mask, scores, -big), axis=2, keepdims=True))
        weights = jnp.where(mask, jnp.exp(scores - top), 0.0)
        total = lax.optimization_barrier(jnp.sum(weights, axis=2))
        rounded = weights.astype(jnp.bfloat16).astype(jnp.float32)
        both_values = jnp.concatenate([all_values, v_rows], axis=0)
        summed = jnp.einsum('hqk,khd->hqd', rounded, both_values)
        attended = (summed / total[..., None]).astype(jnp.bfloat16)
        return jnp.transpose(attended, (1, 0, 2)).reshape(SUF_DEV, D)
    attended = lax.map(one_row, jnp.arange(BLOCKS, dtype=jnp.int32)).reshape(TOKENS, D)
    branch = jnp.dot(attended, w_out, preferred_element_type=jnp.float32)
    return (inputs + branch).astype(jnp.bfloat16)
```

```python
import functools

import jax
import jax.numpy as jnp
from jax import lax
from jax.experimental import pallas as pl
from jax.experimental.pallas import tpu as pltpu
from jax.sharding import PartitionSpec as P

HD = 128
GROUPS = 4
TAG_ROWS = 16

big = 1e30

VMEM = pl.BlockSpec(memory_space=pltpu.VMEM)
SMEM = pl.BlockSpec(memory_space=pltpu.SMEM)
NT = (((1,), (1,)), ((), ()))
TN = (((0,), (0,)), ((), ()))


def dot(a, b, dims=(((1,), (0,)), ((), ()))):
    return lax.dot_general(a, b, dims, preferred_element_type=jnp.float32)


def head_at(part, shift, heads):
    return lax.rem(part + shift, heads) * HD


def pack_kernel(blocks, heads, part_ref, slot_ref, live_ref, keys_ref, values_ref, *outs):
    rows = keys_ref.shape[1]
    group = lax.div(slot_ref[0] * GROUPS, blocks)
    tag = jnp.where(live_ref[0] == 1, group, -1).astype(jnp.float32)
    tag_rows = jnp.full((TAG_ROWS, HD), tag, jnp.float32).astype(jnp.bfloat16)
    for k in range(heads):
        at = pl.ds(pl.multiple_of(head_at(part_ref[0], k, heads), HD), HD)
        outs[k][0:rows, :] = keys_ref[0, :, at]
        outs[k][rows : 2 * rows, :] = values_ref[0, :, at]
        outs[k][2 * rows : 2 * rows + TAG_ROWS, :] = tag_rows


def query_kernel(
    heads,
    part_ref,
    request_group_ref,
    hidden_ref,
    gain_ref,
    bias_ref,
    w_query_ref,
    segment_ref,
    normed_ref,
    query_ref,
    *outs,
):
    rows = hidden_ref.shape[0]
    inputs = hidden_ref[...].astype(jnp.float32)
    mean = jnp.mean(inputs, axis=-1, keepdims=True)
    centred = inputs - mean
    var = jnp.mean(centred * centred, axis=-1, keepdims=True)
    normed = centred * lax.rsqrt(var + 1e-05) * gain_ref[...] + bias_ref[...]
    normed = normed.astype(jnp.bfloat16)
    normed_ref[...] = normed
    query = dot(normed, w_query_ref[...]) * (HD**-0.5)
    query_ref[...] = query.astype(jnp.bfloat16)
    segment = segment_ref[...]
    group = jnp.zeros_like(segment)
    for r in range(request_group_ref.shape[1]):
        group = jnp.where(segment == r, request_group_ref[0, r], group)
    group_rows = jnp.broadcast_to(group.astype(jnp.float32), (TAG_ROWS, rows))
    for k in range(heads):
        at = pl.ds(pl.multiple_of(head_at(part_ref[0], k, heads), HD), HD)
        outs[k][0:rows, :] = query_ref[:, at]
        outs[k][rows : rows + TAG_ROWS, :] = group_rows.astype(jnp.bfloat16)


def suffix_kernel(
    heads, normed_ref, query_ref, w_key_ref, w_value_ref, segment_ref, sum_ref, log_ref
):
    rows = normed_ref.shape[0]
    key = dot(normed_ref[...], w_key_ref[...]).astype(jnp.bfloat16)
    value = dot(normed_ref[...], w_value_ref[...]).astype(jnp.bfloat16)
    by_token = jnp.broadcast_to(segment_ref[...], (rows, rows))
    key_place = lax.broadcasted_iota(jnp.int32, (rows, rows), 0)
    token_place = lax.broadcasted_iota(jnp.int32, (rows, rows), 1)
    by_key = jnp.sum(
        jnp.where(key_place == token_place, by_token, 0).astype(jnp.float32), axis=1, keepdims=True
    )
    mask = (by_key == by_token.astype(jnp.float32)) & (key_place <= token_place)
    for h in range(heads):
        cols = slice(h * HD, (h + 1) * HD)
        scores = jnp.where(mask, dot(key[:, cols], query_ref[:, cols], NT), -big)
        top = jnp.max(scores, axis=0, keepdims=True)
        weights = jnp.exp(scores - top)
        total = jnp.sum(weights, axis=0, keepdims=True)
        summed = dot(value[:, cols], weights.astype(jnp.bfloat16), TN)
        sum_ref[cols, :] = summed / total
        log_ref[h : h + 1, :] = top + jnp.log(total)


def prefix_kernel(n_queries, n_blocks, rows, *refs):
    queries = refs[:n_queries]
    blocks = refs[n_queries : n_queries + n_blocks]
    outs = refs[n_queries + n_blocks : 2 * n_queries + n_blocks]
    query = jnp.concatenate([ref[0:rows, :] for ref in queries], axis=0)
    group = jnp.concatenate(
        [ref[rows : rows + TAG_ROWS, :].astype(jnp.float32)[0:1, :] for ref in queries], axis=1
    )
    tokens = query.shape[0]
    key_rows = (HD, 2 * HD + TAG_ROWS)
    step = key_rows[1]

    def score(ref, at):
        keys = ref[pl.ds(at, HD), :]
        tag = ref[pl.ds(at + 2 * HD, TAG_ROWS), :].astype(jnp.float32)[0:1, 0:1]
        scores = dot(keys, query, NT)
        return scores, group == tag

    def absorb(carry, found):
        top, total, summed = carry
        new_top = top
        for scores, mask, _ in found:
            best = jnp.max(scores, axis=0, keepdims=True)
            new_top = jnp.maximum(new_top, jnp.where(mask, best, -big))
        factor = jnp.exp(top - new_top)
        total, summed = total * factor, summed * factor
        for scores, mask, values in found:
            weights = jnp.exp(scores - jnp.where(mask, new_top, big))
            total = total + jnp.sum(weights, axis=0, keepdims=True)
            summed = summed + dot(values, weights.astype(jnp.bfloat16), TN)
        return new_top, total, summed

    def one(ref, at):
        scores, mask = score(ref, at)
        return scores, mask, ref[pl.ds(at + HD, HD), :]

    carry = (
        jnp.full((1, tokens), -big, jnp.float32),
        jnp.zeros((1, tokens), jnp.float32),
        jnp.zeros((HD, tokens), jnp.float32),
    )
    carry = absorb(carry, [one(ref, 0) for ref in blocks if ref.shape[0] == step])
    for ref in blocks:
        held = ref.shape[0] // step
        if held > 1:

            def body(i, state, ref=ref):
                return absorb(state, [one(ref, pl.multiple_of(i * step, TAG_ROWS))])

            carry = lax.fori_loop(0, held, body, carry)
    top, total, summed = carry
    found = total > 0.0
    summed = summed * jnp.where(found, 1.0 / jnp.where(found, total, 1.0), 0.0)
    log = jnp.where(found, top + jnp.log(jnp.where(found, total, 1.0)), -big)
    first = log.astype(jnp.bfloat16).astype(jnp.float32)
    second = (log - first).astype(jnp.bfloat16).astype(jnp.float32)
    third = log - first - second
    place = lax.broadcasted_iota(jnp.int32, (TAG_ROWS, tokens), 0)
    logs = jnp.where(place == 0, first, jnp.where(place == 1, second, jnp.where(place == 2, third, 0.0)))
    for k in range(n_queries):
        cols = slice(k * rows, (k + 1) * rows)
        outs[k][0:HD, :] = summed[:, cols].astype(jnp.bfloat16)
        outs[k][HD : HD + TAG_ROWS, :] = logs[:, cols].astype(jnp.bfloat16)


def project_kernel(heads, part_ref, half_ref, sum_ref, log_ref, w_out_ref, *refs):
    backs = refs[:heads]
    keep_ref, send_ref, attended, branch = refs[heads:]
    for k in range(heads):
        at = pl.multiple_of(head_at(part_ref[0], k, heads), HD)
        logs = backs[k][HD : HD + TAG_ROWS, :].astype(jnp.float32)
        prefix_log = logs[0:1, :] + logs[1:2, :] + logs[2:3, :]
        suffix_log = log_ref[pl.ds(lax.rem(part_ref[0] + k, heads), 1), :]
        top = jnp.maximum(prefix_log, suffix_log)
        prefix_part = jnp.exp(prefix_log - top)
        suffix_part = jnp.exp(suffix_log - top)
        whole = prefix_part + suffix_part
        joined = (
            backs[k][0:HD, :].astype(jnp.float32) * (prefix_part / whole)
            + sum_ref[pl.ds(at, HD), :] * (suffix_part / whole)
        )
        attended[pl.ds(at, HD), :] = joined.astype(jnp.bfloat16)
    branch[...] = dot(attended[...], w_out_ref[...], TN)
    half = keep_ref.shape[0]
    mine = pl.multiple_of(half_ref[0] * half, half)
    other = pl.multiple_of((1 - half_ref[0]) * half, half)
    keep_ref[...] = branch[pl.ds(mine, half), :]
    send_ref[...] = branch[pl.ds(other, half), :].astype(jnp.bfloat16)


def call(kernel, outs, specs, scratch=()):
    return pl.pallas_call(
        kernel,
        out_shape=tuple(jax.ShapeDtypeStruct(s, t) for s, t in outs),
        in_specs=specs,
        out_specs=(VMEM,) * len(outs),
        scratch_shapes=scratch,
        compiler_params=pltpu.CompilerParams(vmem_limit_bytes=40 * 1024 * 1024),
    )


def local(
    hidden_in,
    norm_gain,
    norm_bias,
    w_query,
    w_key,
    w_value,
    w_out,
    prefix_keys,
    prefix_values,
    segment,
    request_group,
    block_slot,
    block_live,
):
    bf16, f32 = jnp.bfloat16, jnp.float32
    rows, width = hidden_in.shape
    local_width = w_query.shape[1]
    heads = local_width // HD
    n_blk = lax.axis_size("blk")
    n_mp = lax.axis_size("mp")
    rest = n_blk // heads
    me = lax.axis_index("blk")
    part = (me // rest).astype(jnp.int32).reshape(1)
    half = lax.rem(lax.axis_index("mp"), 2).astype(jnp.int32).reshape(1)

    def along_part(x, shift):
        if shift % heads == 0:
            return x
        pairs = [(i, (i // rest + shift) % heads * rest + i % rest) for i in range(n_blk)]
        return lax.ppermute(x, "blk", pairs)

    def across(x, bit):
        return lax.ppermute(x, "blk", [(i, i ^ bit) for i in range(n_blk)])

    def across_mp(x, bit):
        return lax.ppermute(x, "mp", [(i, i ^ bit) for i in range(n_mp)])

    block = 2 * HD + TAG_ROWS
    packs = call(
        functools.partial(pack_kernel, n_blk, heads),
        [((block, HD), bf16)] * heads,
        (SMEM,) * 3 + (VMEM,) * 2,
    )(part, block_slot, block_live, prefix_keys, prefix_values)
    blocks = [along_part(packs[k], k) for k in range(heads)]

    normed, query, *asks = call(
        functools.partial(query_kernel, heads),
        [((rows, width), bf16), ((rows, local_width), bf16)] + [((rows + TAG_ROWS, HD), bf16)] * heads,
        (SMEM,) * 2 + (VMEM,) * 5,
    )(
        part,
        request_group,
        hidden_in,
        norm_gain.reshape(1, width),
        norm_bias.reshape(1, width),
        w_query,
        segment,
    )
    asks = [along_part(asks[k], k) for k in range(heads)]

    bit = 1
    while bit < rest:
        sends = blocks if bit == 1 else [jnp.concatenate(blocks, axis=0)]
        blocks = blocks + [across(x, bit) for x in sends]
        bit *= 2

    suffix_sum, suffix_log = call(
        functools.partial(suffix_kernel, heads),
        [((local_width, rows), f32), ((max(heads, 8), rows), f32)],
        (VMEM,) * 5,
    )(normed, query, w_key, w_value, segment)

    backs = call(
        functools.partial(prefix_kernel, heads, len(blocks), rows),
        [((HD + TAG_ROWS, rows), bf16)] * heads,
        (VMEM,) * (heads + len(blocks)),
    )(*asks, *blocks)
    backs = [along_part(backs[k], -k) for k in range(heads)]

    keep, send = call(
        functools.partial(project_kernel, heads),
        [((rows // 2, width), f32), ((rows // 2, width), bf16)],
        (SMEM,) * 2 + (VMEM,) * (3 + heads),
        scratch=[pltpu.VMEM((local_width, rows), bf16), pltpu.VMEM((rows, width), f32)],
    )(part, half, suffix_sum, suffix_log, w_out, *backs)

    mine = (keep + across_mp(send, 1).astype(f32)).astype(bf16)
    bit = 2
    while bit < n_mp:
        mine = (mine.astype(f32) + across_mp(mine, bit).astype(f32)).astype(bf16 if 2 * bit < n_mp else f32)
        bit *= 2
    inputs = lax.dynamic_slice_in_dim(hidden_in, half[0] * (rows // 2), rows // 2, 0)
    done = (inputs.astype(f32) + mine.astype(f32)).astype(bf16)
    other = across_mp(done, 1)
    first = half[0] == 0
    return jnp.concatenate([jnp.where(first, done, other), jnp.where(first, other, done)], axis=0)


def solution(mesh):
    return jax.shard_map(
        local,
        mesh=mesh,
        in_specs=(
            P("blk", None),
            P(),
            P(),
            P(None, "mp"),
            P(None, "mp"),
            P(None, "mp"),
            P("mp", None),
            P("blk", None, "mp"),
            P("blk", None, "mp"),
            P("blk", None),
            P("blk", None),
            P("blk"),
            P("blk"),
        ),
        out_specs=P("blk", None),
        check_vma=False,
    )
```

```python
import functools

import jax
import jax.numpy as jnp
from jax import lax
from jax.experimental import pallas as pl
from jax.experimental.pallas import tpu as pltpu
from jax.sharding import PartitionSpec as P

HD = 128
GROUPS = 4
NOTE_ROWS = 16
NOTES = 2 * HD
W_CUTS = 4

big = 1e30

VMEM = pl.BlockSpec(memory_space=pltpu.VMEM)
HBM = pl.BlockSpec(memory_space=pltpu.HBM)
NT = (((1,), (1,)), ((), ()))
TN = (((0,), (0,)), ((), ()))


def dot(a, b, dims=(((1,), (0,)), ((), ()))):
    return lax.dot_general(a, b, dims, preferred_element_type=jnp.float32)


def head_at(rest, shift, heads):
    part = lax.div(lax.axis_index("blk"), rest)
    return pl.multiple_of(lax.rem(part + shift, heads) * HD, HD)


def start_all(pairs, sems):
    copies = [pltpu.make_async_copy(a, b, sems.at[i]) for i, (a, b) in enumerate(pairs)]
    for copy in copies:
        copy.start()
    return copies


def front_kernel(heads, rest, *refs):
    keys_ref, values_ref, tag_ref, sources = refs[0], refs[1], refs[2], refs[3:9]
    normed_ref, query_ref = refs[9:11]
    outs, held, sems = refs[11 : 11 + heads], refs[11 + heads : -1], refs[-1]
    hidden_ref, w_query_ref, gain_ref, bias_ref, segment_ref, request_group_ref = held
    rows = hidden_ref.shape[0]
    pairs = list(zip(sources, held))
    for k in range(heads):
        at = pl.ds(head_at(rest, k, heads), HD)
        pairs.append((keys_ref.at[0, :, at], outs[k].at[0:HD, :]))
        pairs.append((values_ref.at[0, :, at], outs[k].at[HD : 2 * HD, :]))
    copies = start_all(pairs, sems)
    copies[0].wait()
    inputs = hidden_ref[...].astype(jnp.float32)
    mean = jnp.mean(inputs, axis=-1, keepdims=True)
    centred = inputs - mean
    var = jnp.mean(centred * centred, axis=-1, keepdims=True)
    copies[2].wait()
    copies[3].wait()
    normed = centred * lax.rsqrt(var + 1e-05) * gain_ref[...] + bias_ref[...]
    normed = normed.astype(jnp.bfloat16)
    normed_ref[...] = normed
    copies[4].wait()
    copies[5].wait()
    segment = segment_ref[...]
    group = jnp.zeros_like(segment)
    for r in range(request_group_ref.shape[1]):
        group = jnp.where(segment == r, request_group_ref[0, r], group)
    tag = tag_ref[...].astype(jnp.float32)
    place = lax.broadcasted_iota(jnp.int32, tag.shape, 0)
    notes = jnp.where(place == 0, tag, group.astype(jnp.float32)).astype(jnp.bfloat16)
    copies[1].wait()
    query = dot(normed, w_query_ref[...]) * (HD**-0.5)
    query_ref[...] = query.astype(jnp.bfloat16)
    for k in range(heads):
        at = pl.ds(head_at(rest, k, heads), HD)
        outs[k][NOTES : NOTES + NOTE_ROWS, :] = notes
        outs[k][NOTES + NOTE_ROWS : NOTES + NOTE_ROWS + rows, :] = query_ref[:, at]
    for copy in copies[6:]:
        copy.wait()


def suffix_kernel(heads, normed_ref, query_ref, *refs):
    sources, (sum_ref, log_ref), held, sems = refs[:3], refs[3:5], refs[5:8], refs[8]
    segment_ref, w_key_ref, w_value_ref = held
    rows, width = normed_ref.shape
    cut = width // W_CUTS
    pairs = [(sources[0], held[0])]
    for source, target in zip(sources[1:], held[1:]):
        pairs += [(source.at[pl.ds(i * cut, cut), :], target.at[pl.ds(i * cut, cut), :]) for i in range(W_CUTS)]
    copies = start_all(pairs, sems)

    def project(target, waits):
        out = jnp.zeros((rows, target.shape[1]), jnp.float32)
        for i, copy in enumerate(waits):
            copy.wait()
            at = slice(i * cut, (i + 1) * cut)
            out = out + dot(normed_ref[:, at], target[at, :])
        return out.astype(jnp.bfloat16)

    key = project(w_key_ref, copies[1 : 1 + W_CUTS])
    value = project(w_value_ref, copies[1 + W_CUTS :])
    copies[0].wait()
    by_token = jnp.broadcast_to(segment_ref[...], (rows, rows))
    key_place = lax.broadcasted_iota(jnp.int32, (rows, rows), 0)
    token_place = lax.broadcasted_iota(jnp.int32, (rows, rows), 1)
    by_key = jnp.sum(
        jnp.where(key_place == token_place, by_token, 0).astype(jnp.float32), axis=1, keepdims=True
    )
    mask = (by_key == by_token.astype(jnp.float32)) & (key_place <= token_place)
    for h in range(heads):
        cols = slice(h * HD, (h + 1) * HD)
        scores = jnp.where(mask, dot(key[:, cols], query_ref[:, cols], NT), -big)
        top = jnp.max(scores, axis=0, keepdims=True)
        weights = jnp.exp(scores - top)
        total = jnp.sum(weights, axis=0, keepdims=True)
        summed = dot(value[:, cols], weights.astype(jnp.bfloat16), TN)
        sum_ref[cols, :] = summed / total
        log_ref[h : h + 1, :] = top + jnp.log(total)


def prefix_kernel(n_queries, n_blocks, rows, *refs):
    blocks, outs = refs[:n_blocks], refs[n_blocks : n_blocks + n_queries]
    step = NOTES + NOTE_ROWS + rows
    query = jnp.concatenate([ref[NOTES + NOTE_ROWS : step, :] for ref in blocks[:n_queries]], axis=0)
    group = jnp.concatenate(
        [
            ref[NOTES : NOTES + NOTE_ROWS, :].astype(jnp.float32)[1:2, :]
            for ref in blocks[:n_queries]
        ],
        axis=1,
    )
    tokens = query.shape[0]

    def one(ref, at):
        tag = ref[pl.ds(at + NOTES, NOTE_ROWS), :].astype(jnp.float32)[0:1, 0:1]
        return dot(ref[pl.ds(at, HD), :], query, NT), group == tag, ref[pl.ds(at + HD, HD), :]

    def absorb(carry, found):
        top, total, summed = carry
        new_top = top
        for scores, mask, _ in found:
            best = jnp.max(scores, axis=0, keepdims=True)
            new_top = jnp.maximum(new_top, jnp.where(mask, best, -big))
        factor = jnp.exp(top - new_top)
        total, summed = total * factor, summed * factor
        for scores, mask, values in found:
            weights = jnp.exp(scores - jnp.where(mask, new_top, big))
            total = total + jnp.sum(weights, axis=0, keepdims=True)
            summed = summed + dot(values, weights.astype(jnp.bfloat16), TN)
        return new_top, total, summed

    carry = (
        jnp.full((1, tokens), -big, jnp.float32),
        jnp.zeros((1, tokens), jnp.float32),
        jnp.zeros((HD, tokens), jnp.float32),
    )
    carry = absorb(carry, [one(ref, 0) for ref in blocks if ref.shape[0] == step])
    for ref in blocks:
        held = ref.shape[0] // step
        if held > 1:

            def body(i, state, ref=ref):
                return absorb(state, [one(ref, pl.multiple_of(i * step, NOTE_ROWS))])

            carry = lax.fori_loop(0, held, body, carry)
    top, total, summed = carry
    found = total > 0.0
    summed = summed * jnp.where(found, 1.0 / jnp.where(found, total, 1.0), 0.0)
    log = jnp.where(found, top + jnp.log(jnp.where(found, total, 1.0)), -big)
    first = log.astype(jnp.bfloat16).astype(jnp.float32)
    second = (log - first).astype(jnp.bfloat16).astype(jnp.float32)
    third = log - first - second
    place = lax.broadcasted_iota(jnp.int32, (NOTE_ROWS, tokens), 0)
    logs = jnp.where(place == 0, first, jnp.where(place == 1, second, jnp.where(place == 2, third, 0.0)))
    for k in range(n_queries):
        cols = slice(k * rows, (k + 1) * rows)
        outs[k][0:HD, :] = summed[:, cols].astype(jnp.bfloat16)
        outs[k][HD : HD + NOTE_ROWS, :] = logs[:, cols].astype(jnp.bfloat16)


def project_kernel(heads, rest, sum_ref, log_ref, w_out_ref, *refs):
    backs = refs[:heads]
    keep_ref, send_ref, attended, branch = refs[heads:]
    for k in range(heads):
        at = head_at(rest, k, heads)
        logs = backs[k][HD : HD + NOTE_ROWS, :].astype(jnp.float32)
        prefix_log = logs[0:1, :] + logs[1:2, :] + logs[2:3, :]
        suffix_log = log_ref[pl.ds(lax.div(at, HD), 1), :]
        top = jnp.maximum(prefix_log, suffix_log)
        prefix_part = jnp.exp(prefix_log - top)
        suffix_part = jnp.exp(suffix_log - top)
        whole = prefix_part + suffix_part
        joined = (
            backs[k][0:HD, :].astype(jnp.float32) * (prefix_part / whole)
            + sum_ref[pl.ds(at, HD), :] * (suffix_part / whole)
        )
        attended[pl.ds(at, HD), :] = joined.astype(jnp.bfloat16)
    branch[...] = dot(attended[...], w_out_ref[...], TN)
    half = keep_ref.shape[0]
    side = lax.rem(lax.axis_index("mp"), 2)
    mine = pl.multiple_of(side * half, half)
    other = pl.multiple_of((1 - side) * half, half)
    keep_ref[...] = branch[pl.ds(mine, half), :]
    send_ref[...] = branch[pl.ds(other, half), :].astype(jnp.bfloat16)


def call(kernel, outs, specs, scratch=()):
    def run(*args):
        pinned = [
            pltpu.with_memory_space_constraint(x, pltpu.HBM) if spec is HBM else x
            for x, spec in zip(args, specs)
        ]
        return inner(*pinned)

    inner = pl.pallas_call(
        kernel,
        out_shape=tuple(jax.ShapeDtypeStruct(s, t) for s, t in outs),
        in_specs=specs,
        out_specs=(VMEM,) * len(outs),
        scratch_shapes=scratch,
        compiler_params=pltpu.CompilerParams(vmem_limit_bytes=40 * 1024 * 1024),
    )
    return run


def local(
    hidden_in,
    norm_gain,
    norm_bias,
    w_query,
    w_key,
    w_value,
    w_out,
    prefix_keys,
    prefix_values,
    segment,
    request_group,
    block_slot,
    block_live,
):
    bf16, f32, i32 = jnp.bfloat16, jnp.float32, jnp.int32
    rows, width = hidden_in.shape
    local_width = w_query.shape[1]
    heads = local_width // HD
    n_blk = lax.axis_size("blk")
    n_mp = lax.axis_size("mp")
    rest = n_blk // heads
    side = lax.rem(lax.axis_index("mp"), 2)

    def exchange(x, shift, back=False):
        pairs = []
        for i in range(n_blk):
            part, place, lane = i // rest, i % rest // 2, i % 2
            for m in range(n_mp):
                other, core = m // 2, m % 2
                blk = (part + shift) % heads * rest + place * 2 + core
                pair = (i * n_mp + m, blk * n_mp + other * 2 + 1 - lane)
                pairs.append(pair[::-1] if back else pair)
        return lax.ppermute(x, ("blk", "mp"), pairs)

    def across(x, bit):
        return lax.ppermute(x, "blk", [(i, i ^ bit) for i in range(n_blk)])

    def across_mp(x, bit):
        return lax.ppermute(x, "mp", [(i, i ^ bit) for i in range(n_mp)])

    group = jnp.where(block_live == 1, block_slot * GROUPS // n_blk, -1).astype(bf16)
    normed, query, *packs = call(
        functools.partial(front_kernel, heads, rest),
        [((rows, width), bf16), ((rows, local_width), bf16)]
        + [((NOTES + NOTE_ROWS + rows, HD), bf16)] * heads,
        (HBM, HBM, VMEM) + (HBM,) * 6,
        [
            pltpu.VMEM((rows, width), bf16),
            pltpu.VMEM(w_query.shape, bf16),
            pltpu.VMEM((1, width), f32),
            pltpu.VMEM((1, width), f32),
            pltpu.VMEM(segment.shape, i32),
            pltpu.SMEM(request_group.shape, i32),
            pltpu.SemaphoreType.DMA((6 + 2 * heads,)),
        ],
    )(
        prefix_keys,
        prefix_values,
        jnp.broadcast_to(group, (NOTE_ROWS, HD)),
        hidden_in,
        w_query,
        norm_gain.reshape(1, width),
        norm_bias.reshape(1, width),
        segment,
        request_group,
    )
    blocks = [exchange(packs[k], k) for k in range(heads)]
    suffix_sum, suffix_log = call(
        functools.partial(suffix_kernel, heads),
        [((local_width, rows), f32), ((max(heads, 8), rows), f32)],
        (VMEM,) * 2 + (HBM,) * 3,
        [
            pltpu.VMEM(segment.shape, i32),
            pltpu.VMEM(w_key.shape, bf16),
            pltpu.VMEM(w_value.shape, bf16),
            pltpu.SemaphoreType.DMA((1 + 2 * W_CUTS,)),
        ],
    )(normed, query, segment, w_key, w_value)
    blocks, suffix_sum, suffix_log = lax.optimization_barrier((blocks, suffix_sum, suffix_log))
    blocks = blocks + [across_mp(x, 1) for x in blocks]
    bit = 2
    while bit < rest:
        blocks = blocks + [across(jnp.concatenate(blocks, axis=0), bit)]
        bit *= 2

    backs = call(
        functools.partial(prefix_kernel, heads, len(blocks), rows),
        [((HD + NOTE_ROWS, rows), bf16)] * heads,
        (VMEM,) * len(blocks),
    )(*blocks)
    backs = [exchange(backs[k], k, back=True) for k in range(heads)]

    keep, send = call(
        functools.partial(project_kernel, heads, rest),
        [((rows // 2, width), f32), ((rows // 2, width), bf16)],
        (VMEM,) * (3 + heads),
        [pltpu.VMEM((local_width, rows), bf16), pltpu.VMEM((rows, width), f32)],
    )(suffix_sum, suffix_log, w_out, *backs)

    mine = (keep + across_mp(send, 1).astype(f32)).astype(bf16)
    bit = 2
    while bit < n_mp:
        mine = (mine.astype(f32) + across_mp(mine, bit).astype(f32)).astype(bf16 if 2 * bit < n_mp else f32)
        bit *= 2
    inputs = lax.dynamic_slice_in_dim(hidden_in, side * (rows // 2), rows // 2, 0)
    done = (inputs.astype(f32) + mine.astype(f32)).astype(bf16)
    other = across_mp(done, 1)
    first = side == 0
    return jnp.concatenate([jnp.where(first, done, other), jnp.where(first, other, done)], axis=0)


def solution(mesh):
    return jax.shard_map(
        local,
        mesh=mesh,
        in_specs=(
            P("blk", None),
            P(),
            P(),
            P(None, "mp"),
            P(None, "mp"),
            P(None, "mp"),
            P("mp", None),
            P("blk", None, "mp"),
            P("blk", None, "mp"),
            P("blk", None),
            P("blk", None),
            P("blk"),
            P("blk"),
        ),
        out_specs=P("blk", None),
        check_vma=False,
    )
```

```python
import functools

import jax
import jax.numpy as jnp
from jax import lax
from jax.experimental import pallas as pl
from jax.experimental.pallas import tpu as pltpu
from jax.sharding import PartitionSpec as P

HD = 128
GROUPS = 4
NOTE_ROWS = 16
ASK_ROWS = NOTE_ROWS + 128
W_CUTS = 4
ROW_CUTS = 2

big = 1e30

VMEM = pl.BlockSpec(memory_space=pltpu.VMEM)
HBM = pl.BlockSpec(memory_space=pltpu.HBM)
NT = (((1,), (1,)), ((), ()))
TN = (((0,), (0,)), ((), ()))


def dot(a, b, dims=(((1,), (0,)), ((), ()))):
    return lax.dot_general(a, b, dims, preferred_element_type=jnp.float32)


def head_at(rest, bits):
    part = lax.div(lax.axis_index("blk"), rest)
    return pl.multiple_of((part ^ bits) * HD, HD)


def start_all(pairs, sems):
    copies = [pltpu.make_async_copy(a, b, sems.at[i]) for i, (a, b) in enumerate(pairs)]
    for copy in copies:
        copy.start()
    return copies


def block_copies(rest, bits, keys_ref, values_ref, out, at):
    cols = pl.ds(head_at(rest, bits), HD)
    return [
        (keys_ref.at[0, :, cols], out.at[at : at + HD, :]),
        (values_ref.at[0, :, cols], out.at[at + HD : at + 2 * HD, :]),
    ]


def query_kernel(heads, rest, *refs):
    keys_ref, values_ref, tag_ref, hidden_in, w_query, *sources = refs[:9]
    normed_ref, query_ref = refs[9:11]
    outs, held, sems = refs[11 : 11 + heads], refs[11 + heads : -1], refs[-1]
    hidden_ref, w_query_ref, gain_ref, bias_ref, segment_ref, request_group_ref = held
    rows, width = hidden_ref.shape
    row_cuts = [pl.ds(i * (rows // ROW_CUTS), rows // ROW_CUTS) for i in range(ROW_CUTS)]
    w_cuts = [pl.ds(i * (width // W_CUTS), width // W_CUTS) for i in range(W_CUTS)]
    pairs = [(hidden_in.at[cut, :], hidden_ref.at[cut, :]) for cut in row_cuts]
    pairs += list(zip(sources, held[2:]))
    pairs += [(w_query.at[cut, :], w_query_ref.at[cut, :]) for cut in w_cuts]
    for k, out in enumerate(outs):
        pairs += block_copies(rest, k, keys_ref, values_ref, out, NOTE_ROWS + rows)
    copies = start_all(pairs, sems)
    small = copies[ROW_CUTS : ROW_CUTS + 4]
    weights = copies[ROW_CUTS + 4 : ROW_CUTS + 4 + W_CUTS]
    for cut, copy in zip(row_cuts, copies):
        copy.wait()
        if cut is row_cuts[0]:
            small[0].wait()
            small[1].wait()
        inputs = hidden_ref[cut, :].astype(jnp.float32)
        mean = jnp.mean(inputs, axis=-1, keepdims=True)
        centred = inputs - mean
        var = jnp.mean(centred * centred, axis=-1, keepdims=True)
        normed = centred * lax.rsqrt(var + 1e-05) * gain_ref[...] + bias_ref[...]
        normed_ref[cut, :] = normed.astype(jnp.bfloat16)
    small[2].wait()
    small[3].wait()
    segment = segment_ref[...]
    group = jnp.zeros_like(segment)
    for r in range(request_group_ref.shape[1]):
        group = jnp.where(segment == r, request_group_ref[0, r], group)
    tag = tag_ref[...].astype(jnp.float32)
    place = lax.broadcasted_iota(jnp.int32, tag.shape, 0)
    notes = jnp.where(place == 0, tag, group.astype(jnp.float32)).astype(jnp.bfloat16)
    query = jnp.zeros(query_ref.shape, jnp.float32)
    for cut, copy in zip(w_cuts, weights):
        copy.wait()
        query = query + dot(normed_ref[:, cut], w_query_ref[cut, :])
    query_ref[...] = (query * (HD**-0.5)).astype(jnp.bfloat16)
    for k, out in enumerate(outs):
        out[0:NOTE_ROWS, :] = notes
        out[NOTE_ROWS : NOTE_ROWS + rows, :] = query_ref[:, pl.ds(head_at(rest, k), HD)]
    for copy in copies[ROW_CUTS + 4 + W_CUTS :]:
        copy.wait()


def suffix_kernel(heads, normed_ref, query_ref, *refs):
    sources, (sum_ref, log_ref), held, sems = refs[:3], refs[3:5], refs[5:8], refs[8]
    segment_ref, w_key_ref, w_value_ref = held
    rows, width = normed_ref.shape
    cut = width // W_CUTS
    pairs = [(sources[0], held[0])]
    for source, target in zip(sources[1:], held[1:]):
        parts = [pl.ds(i * cut, cut) for i in range(W_CUTS)]
        pairs += [(source.at[part, :], target.at[part, :]) for part in parts]
    copies = start_all(pairs, sems)

    def project(target, waits):
        out = jnp.zeros((rows, target.shape[1]), jnp.float32)
        for i, copy in enumerate(waits):
            copy.wait()
            at = slice(i * cut, (i + 1) * cut)
            out = out + dot(normed_ref[:, at], target[at, :])
        return out.astype(jnp.bfloat16)

    key = project(w_key_ref, copies[1 : 1 + W_CUTS])
    value = project(w_value_ref, copies[1 + W_CUTS :])
    copies[0].wait()
    by_token = jnp.broadcast_to(segment_ref[...], (rows, rows))
    key_place = lax.broadcasted_iota(jnp.int32, (rows, rows), 0)
    token_place = lax.broadcasted_iota(jnp.int32, (rows, rows), 1)
    by_key = jnp.sum(
        jnp.where(key_place == token_place, by_token, 0).astype(jnp.float32), axis=1, keepdims=True
    )
    mask = (by_key == by_token.astype(jnp.float32)) & (key_place <= token_place)
    for h in range(heads):
        cols = slice(h * HD, (h + 1) * HD)
        scores = jnp.where(mask, dot(key[:, cols], query_ref[:, cols], NT), -big)
        top = jnp.max(scores, axis=0, keepdims=True)
        weights = jnp.exp(scores - top)
        total = jnp.sum(weights, axis=0, keepdims=True)
        summed = dot(value[:, cols], weights.astype(jnp.bfloat16), TN)
        sum_ref[cols, :] = summed / total
        log_ref[h : h + 1, :] = top + jnp.log(total)


def absorb(carry, found):
    top, total, summed = carry
    new_top = top
    for scores, mask, _ in found:
        best = jnp.max(scores, axis=0, keepdims=True)
        new_top = jnp.maximum(new_top, jnp.where(mask, best, -big))
    factor = jnp.exp(top - new_top)
    total, summed = total * factor, summed * factor
    for scores, mask, values in found:
        weights = jnp.exp(scores - jnp.where(mask, new_top, big))
        total = total + jnp.sum(weights, axis=0, keepdims=True)
        summed = summed + dot(values, weights.astype(jnp.bfloat16), TN)
    return new_top, total, summed


def questions(asks, rows):
    query = jnp.concatenate([ref[NOTE_ROWS : NOTE_ROWS + rows, :] for ref in asks], axis=0)
    notes = [ref[0:NOTE_ROWS, :].astype(jnp.float32) for ref in asks]
    return query, jnp.concatenate([note[1:2, :] for note in notes], axis=1), notes


def first_kernel(rows, *refs):
    asks, (state_ref, sum_ref) = refs[:-2], refs[-2:]
    query, group, notes = questions(asks, rows)
    tokens = query.shape[0]
    found = []
    at = NOTE_ROWS + rows
    for ref, note in zip(asks, notes):
        scores = dot(ref[at : at + HD, :], query, NT)
        found.append((scores, group == note[0:1, 0:1], ref[at + HD : at + 2 * HD, :]))
    carry = (
        jnp.full((1, tokens), -big, jnp.float32),
        jnp.zeros((1, tokens), jnp.float32),
        jnp.zeros((HD, tokens), jnp.float32),
    )
    top, total, summed = absorb(carry, found)
    state_ref[0:1, :] = top
    state_ref[1:2, :] = total
    sum_ref[...] = summed


def second_kernel(rows, n_asks, *refs):
    asks, state_ref, sum_ref, notes_ref = refs[:n_asks], *refs[n_asks : n_asks + 3]
    blocks, outs = refs[n_asks + 3 : -n_asks], refs[-n_asks:]
    query, group, _ = questions(asks, rows)
    tokens = query.shape[0]

    def one(ref, at, place):
        tag = notes_ref[pl.ds(place, NOTE_ROWS), :].astype(jnp.float32)[0:1, 0:1]
        return dot(ref[pl.ds(at, HD), :], query, NT), group == tag, ref[pl.ds(at + HD, HD), :]

    carry = (state_ref[0:1, :], state_ref[1:2, :], sum_ref[...])
    singles, place = [], 0
    for ref in blocks:
        held = ref.shape[0] // (2 * HD)
        if held == 1:
            singles.append(one(ref, 0, place))
        place += held * NOTE_ROWS
    carry = absorb(carry, singles)
    place = 0
    for ref in blocks:
        held = ref.shape[0] // (2 * HD)
        if held > 1:

            def body(i, state, ref=ref, place=place):
                at = pl.multiple_of(i * 2 * HD, HD)
                return absorb(state, [one(ref, at, pl.multiple_of(place + i * NOTE_ROWS, NOTE_ROWS))])

            carry = lax.fori_loop(0, held, body, carry)
        place += held * NOTE_ROWS
    top, total, summed = carry
    found = total > 0.0
    summed = summed * jnp.where(found, 1.0 / jnp.where(found, total, 1.0), 0.0)
    log = jnp.where(found, top + jnp.log(jnp.where(found, total, 1.0)), -big)
    first = log.astype(jnp.bfloat16).astype(jnp.float32)
    second = (log - first).astype(jnp.bfloat16).astype(jnp.float32)
    third = log - first - second
    place = lax.broadcasted_iota(jnp.int32, (NOTE_ROWS, tokens), 0)
    logs = jnp.where(place == 0, first, jnp.where(place == 1, second, jnp.where(place == 2, third, 0.0)))
    for k, out in enumerate(outs):
        cols = slice(k * rows, (k + 1) * rows)
        out[0:HD, :] = summed[:, cols].astype(jnp.bfloat16)
        out[HD : HD + NOTE_ROWS, :] = logs[:, cols].astype(jnp.bfloat16)


def project_kernel(rest, order, sum_ref, log_ref, w_out_ref, *refs):
    backs = refs[: len(order)]
    keep_ref, send_ref, attended, branch = refs[len(order) :]
    for bits, back in zip(order, backs):
        at = head_at(rest, bits)
        logs = back[HD : HD + NOTE_ROWS, :].astype(jnp.float32)
        prefix_log = logs[0:1, :] + logs[1:2, :] + logs[2:3, :]
        suffix_log = log_ref[pl.ds(lax.div(at, HD), 1), :]
        top = jnp.maximum(prefix_log, suffix_log)
        prefix_part = jnp.exp(prefix_log - top)
        suffix_part = jnp.exp(suffix_log - top)
        whole = prefix_part + suffix_part
        joined = (
            back[0:HD, :].astype(jnp.float32) * (prefix_part / whole)
            + sum_ref[pl.ds(at, HD), :] * (suffix_part / whole)
        )
        attended[pl.ds(at, HD), :] = joined.astype(jnp.bfloat16)
    branch[...] = dot(attended[...], w_out_ref[...], TN)
    half = keep_ref.shape[0]
    side = lax.rem(lax.axis_index("mp"), 2)
    keep_ref[...] = branch[pl.ds(pl.multiple_of(side * half, half), half), :]
    other = branch[pl.ds(pl.multiple_of((1 - side) * half, half), half), :]
    send_ref[...] = other.astype(jnp.bfloat16)


def own_half_kernel(half_ref, out_ref, sem):
    half = half_ref.shape[0]
    side = lax.rem(lax.axis_index("mp"), 2)
    rows = pl.ds(pl.multiple_of(side * half, half), half)
    copy = pltpu.make_async_copy(half_ref, out_ref.at[rows, :], sem.at[0])
    copy.start()
    copy.wait()


def other_half_kernel(half_ref, _, out_ref, sem):
    half = half_ref.shape[0]
    side = lax.rem(lax.axis_index("mp"), 2)
    rows = pl.ds(pl.multiple_of((1 - side) * half, half), half)
    copy = pltpu.make_async_copy(half_ref, out_ref.at[rows, :], sem.at[0])
    copy.start()
    copy.wait()


def call(kernel, outs, specs, scratch=(), out_specs=None, aliases=None):
    def run(*args):
        pinned = [
            pltpu.with_memory_space_constraint(x, pltpu.HBM) if spec is HBM else x
            for x, spec in zip(args, specs)
        ]
        return inner(*pinned)

    inner = pl.pallas_call(
        kernel,
        out_shape=tuple(jax.ShapeDtypeStruct(s, t) for s, t in outs),
        in_specs=specs,
        out_specs=out_specs or (VMEM,) * len(outs),
        scratch_shapes=scratch,
        input_output_aliases=aliases or {},
        compiler_params=pltpu.CompilerParams(vmem_limit_bytes=40 * 1024 * 1024),
    )
    return run


def local(
    hidden_in,
    norm_gain,
    norm_bias,
    w_query,
    w_key,
    w_value,
    w_out,
    prefix_keys,
    prefix_values,
    segment,
    request_group,
    block_slot,
    block_live,
):
    bf16, f32, i32 = jnp.bfloat16, jnp.float32, jnp.int32
    rows, width = hidden_in.shape
    local_width = w_query.shape[1]
    heads = local_width // HD
    n_blk = lax.axis_size("blk")
    n_mp = lax.axis_size("mp")
    rest = n_blk // heads
    side = lax.rem(lax.axis_index("mp"), 2)
    order = tuple(reversed(range(heads)))

    def exchange(x, bits, back=False):
        pairs = []
        for i in range(n_blk):
            part, place, lane = i // rest, i % rest // 2, i % 2
            for m in range(n_mp):
                other, core = m // 2, m % 2
                blk = (part ^ bits) * rest + place * 2 + core
                pair = (i * n_mp + m, blk * n_mp + other * 2 + 1 - lane)
                pairs.append(pair[::-1] if back else pair)
        return lax.ppermute(x, ("blk", "mp"), pairs)

    def across(x, bit):
        return lax.ppermute(x, "blk", [(i, i ^ bit) for i in range(n_blk)])

    def across_mp(x, bit):
        return lax.ppermute(x, "mp", [(i, i ^ bit) for i in range(n_mp)])

    group = jnp.where(block_live == 1, block_slot * GROUPS // n_blk, -1).astype(bf16)
    normed, query, *packs = call(
        functools.partial(query_kernel, heads, rest),
        [((rows, width), bf16), ((rows, local_width), bf16)]
        + [((NOTE_ROWS + rows + 2 * HD, HD), bf16)] * heads,
        (HBM, HBM, VMEM) + (HBM,) * 6,
        [
            pltpu.VMEM((rows, width), bf16),
            pltpu.VMEM(w_query.shape, bf16),
            pltpu.VMEM((1, width), f32),
            pltpu.VMEM((1, width), f32),
            pltpu.VMEM(segment.shape, i32),
            pltpu.SMEM(request_group.shape, i32),
            pltpu.SemaphoreType.DMA((4 + ROW_CUTS + W_CUTS + 2 * heads,)),
        ],
    )(
        prefix_keys,
        prefix_values,
        jnp.broadcast_to(group, (NOTE_ROWS, HD)),
        hidden_in,
        w_query,
        norm_gain.reshape(1, width),
        norm_bias.reshape(1, width),
        segment,
        request_group,
    )
    asks = [exchange(packs[k], k) for k in order]
    suffix_sum, suffix_log = call(
        functools.partial(suffix_kernel, heads),
        [((local_width, rows), f32), ((max(heads, 8), rows), f32)],
        (VMEM,) * 2 + (HBM,) * 3,
        [
            pltpu.VMEM(segment.shape, i32),
            pltpu.VMEM(w_key.shape, bf16),
            pltpu.VMEM(w_value.shape, bf16),
            pltpu.SemaphoreType.DMA((1 + 2 * W_CUTS,)),
        ],
    )(normed, query, segment, w_key, w_value)
    asks, suffix_sum, suffix_log = lax.optimization_barrier((asks, suffix_sum, suffix_log))

    blocks = [x[NOTE_ROWS + rows :] for x in asks]
    notes = jnp.concatenate([x[:NOTE_ROWS] for x in asks], axis=0)
    state, summed = call(
        functools.partial(first_kernel, rows),
        [((8, heads * rows), f32), ((HD, heads * rows), f32)],
        (VMEM,) * heads,
    )(*asks)
    others = [across_mp(x, 1) for x in blocks]
    other_notes = across_mp(notes, 1)
    bit = 2
    while bit < rest:
        everything = jnp.concatenate(blocks + others, axis=0)
        all_notes = jnp.concatenate([notes, other_notes], axis=0)
        others = others + [across(everything, bit)]
        other_notes = jnp.concatenate([other_notes, across(all_notes, bit)], axis=0)
        bit *= 2
    backs = call(
        functools.partial(second_kernel, rows, heads),
        [((HD + NOTE_ROWS, rows), bf16)] * heads,
        (VMEM,) * (heads + 3 + len(others)),
    )(*asks, state, summed, other_notes, *others)
    backs = [exchange(x, k, back=True) for k, x in zip(order, backs)]

    keep, send = call(
        functools.partial(project_kernel, rest, order),
        [((rows // 2, width), f32), ((rows // 2, width), bf16)],
        (VMEM,) * (3 + heads),
        [pltpu.VMEM((local_width, rows), bf16), pltpu.VMEM((rows, width), f32)],
    )(suffix_sum, suffix_log, w_out, *backs)

    mine = (keep + across_mp(send, 1).astype(f32)).astype(bf16)
    bit = 2
    while bit < n_mp:
        mine = (mine.astype(f32) + across_mp(mine, bit).astype(f32)).astype(bf16 if 2 * bit < n_mp else f32)
        bit *= 2
    inputs = lax.dynamic_slice_in_dim(hidden_in, side * (rows // 2), rows // 2, 0)
    done = (inputs.astype(f32) + mine.astype(f32)).astype(bf16)
    other = across_mp(done, 1)
    whole = call(
        own_half_kernel,
        [((rows, width), bf16)],
        (VMEM,),
        [pltpu.SemaphoreType.DMA((1,))],
        (HBM,),
    )(done)[0]
    return call(
        other_half_kernel,
        [((rows, width), bf16)],
        (VMEM, HBM),
        [pltpu.SemaphoreType.DMA((1,))],
        (HBM,),
        {1: 0},
    )(other, whole)[0]


def solution(mesh):
    return jax.shard_map(
        local,
        mesh=mesh,
        in_specs=(
            P("blk", None),
            P(),
            P(),
            P(None, "mp"),
            P(None, "mp"),
            P(None, "mp"),
            P("mp", None),
            P("blk", None, "mp"),
            P("blk", None, "mp"),
            P("blk", None),
            P("blk", None),
            P("blk"),
            P("blk"),
        ),
        out_specs=P("blk", None),
        check_vma=False,
    )
```

```python
import functools

import jax
import jax.numpy as jnp
from jax import lax
from jax.experimental import pallas as pl
from jax.experimental.pallas import tpu as pltpu
from jax.sharding import PartitionSpec as P

HD = 128
GROUPS = 4
NOTE_ROWS = 16
ASK_ROWS = NOTE_ROWS + 128
W_CUTS = 4
ROW_CUTS = 2

ORDER = (1, 0)

big = 1e30
Q = 3
SFX = 10
JOIN = 30

VMEM = pl.BlockSpec(memory_space=pltpu.VMEM)
HBM = pl.BlockSpec(memory_space=pltpu.HBM)
NT = (((1,), (1,)), ((), ()))
TN = (((0,), (0,)), ((), ()))


def dot(a, b, dims=(((1,), (0,)), ((), ()))):
    return lax.dot_general(a, b, dims, preferred_element_type=jnp.float32)


def head_at(bits, i, per):
    pair = lax.rem(lax.div(lax.axis_index("blk"), 2), 2)
    return pl.multiple_of(((pair ^ bits) * per + i) * HD, HD)


def start_all(pairs, sems):
    copies = [pltpu.make_async_copy(a, b, sems.at[i]) for i, (a, b) in enumerate(pairs)]
    for copy in copies:
        copy.start()
    return copies


def block_copies(per, bits, keys_ref, values_ref, out, at):
    pairs = []
    for i in range(per):
        cols = pl.ds(head_at(bits, i, per), HD)
        pairs.append((keys_ref.at[0, :, cols], out.at[at : at + HD, :]))
        pairs.append((values_ref.at[0, :, cols], out.at[at + HD : at + 2 * HD, :]))
        at += 2 * HD
    return pairs


def far_kernel(per, keys_ref, values_ref, tag_ref, *refs):
    outs, sems = refs[:2], refs[2]
    pairs = []
    for bits, out in enumerate(outs):
        pairs += block_copies(per, bits, keys_ref, values_ref, out, 0)
    copies = start_all(pairs, sems)
    for out in outs:
        out[2 * HD * per : 2 * HD * per + NOTE_ROWS, :] = tag_ref[...]
    for copy in copies:
        copy.wait()


def join_kernel(_, *refs):
    out = refs[-1]
    for i, ref in enumerate(refs[:-1]):
        out[i * ref.shape[0] : (i + 1) * ref.shape[0], :] = ref[...]


def query_kernel(per, *refs):
    keys_ref, values_ref, tag_ref, hidden_in, w_query, *sources = refs[:9]
    normed_ref, query_ref = refs[9:11]
    outs, held, sems = refs[11:13], refs[13:-1], refs[-1]
    hidden_ref, w_query_ref, gain_ref, bias_ref, segment_ref, request_group_ref = held
    rows, width = hidden_ref.shape
    row_cuts = [pl.ds(i * (rows // ROW_CUTS), rows // ROW_CUTS) for i in range(ROW_CUTS)]
    w_cuts = [pl.ds(i * (width // W_CUTS), width // W_CUTS) for i in range(W_CUTS)]
    pairs = [(hidden_in.at[cut, :], hidden_ref.at[cut, :]) for cut in row_cuts]
    pairs += list(zip(sources, held[2:]))
    pairs += [(w_query.at[cut, :], w_query_ref.at[cut, :]) for cut in w_cuts]
    for bits, out in enumerate(outs):
        pairs += block_copies(per, bits, keys_ref, values_ref, out, per * rows)
    copies = start_all(pairs, sems)
    small = copies[ROW_CUTS : ROW_CUTS + 4]
    weights = copies[ROW_CUTS + 4 : ROW_CUTS + 4 + W_CUTS]
    for cut, copy in zip(row_cuts, copies):
        copy.wait()
        if cut is row_cuts[0]:
            small[0].wait()
            small[1].wait()
        inputs = hidden_ref[cut, :].astype(jnp.float32)
        mean = jnp.mean(inputs, axis=-1, keepdims=True)
        centred = inputs - mean
        var = jnp.mean(centred * centred, axis=-1, keepdims=True)
        normed = centred * lax.rsqrt(var + 1e-05) * gain_ref[...] + bias_ref[...]
        normed_ref[cut, :] = normed.astype(jnp.bfloat16)
    small[2].wait()
    small[3].wait()
    segment = segment_ref[...]
    group = jnp.zeros_like(segment)
    for r in range(request_group_ref.shape[1]):
        group = jnp.where(segment == r, request_group_ref[0, r], group)
    tag = tag_ref[...].astype(jnp.float32)
    place = lax.broadcasted_iota(jnp.int32, tag.shape, 0)
    notes = jnp.where(place == 0, tag, group.astype(jnp.float32)).astype(jnp.bfloat16)
    query = jnp.zeros(query_ref.shape, jnp.float32)
    for cut, copy in zip(w_cuts, weights):
        copy.wait()
        query = query + dot(normed_ref[:, cut], w_query_ref[cut, :])
    query_ref[...] = (query * (HD**-0.5)).astype(jnp.bfloat16)
    for bits, out in enumerate(outs):
        for i in range(per):
            out[i * rows : (i + 1) * rows, :] = query_ref[:, pl.ds(head_at(bits, i, per), HD)]
        at = per * (rows + 2 * HD)
        out[at : at + NOTE_ROWS, :] = notes
    for copy in copies[ROW_CUTS + 4 + W_CUTS :]:
        copy.wait()


def suffix_kernel(heads, normed_ref, query_ref, *refs):
    sources, (sum_ref, log_ref), held, sems = refs[:3], refs[3:5], refs[5:8], refs[8]
    segment_ref, w_key_ref, w_value_ref = held
    rows, width = normed_ref.shape
    cut = width // W_CUTS
    pairs = [(sources[0], held[0])]
    for source, target in zip(sources[1:], held[1:]):
        parts = [pl.ds(i * cut, cut) for i in range(W_CUTS)]
        pairs += [(source.at[part, :], target.at[part, :]) for part in parts]
    copies = start_all(pairs, sems)

    def project(target, waits):
        out = jnp.zeros((rows, target.shape[1]), jnp.float32)
        for i, copy in enumerate(waits):
            copy.wait()
            at = slice(i * cut, (i + 1) * cut)
            out = out + dot(normed_ref[:, at], target[at, :])
        return out.astype(jnp.bfloat16)

    key = project(w_key_ref, copies[1 : 1 + W_CUTS])
    value = project(w_value_ref, copies[1 + W_CUTS :])
    copies[0].wait()
    by_token = jnp.broadcast_to(segment_ref[...], (rows, rows))
    key_place = lax.broadcasted_iota(jnp.int32, (rows, rows), 0)
    token_place = lax.broadcasted_iota(jnp.int32, (rows, rows), 1)
    by_key = jnp.sum(
        jnp.where(key_place == token_place, by_token, 0).astype(jnp.float32), axis=1, keepdims=True
    )
    mask = (by_key == by_token.astype(jnp.float32)) & (key_place <= token_place)
    for h in range(heads):
        cols = slice(h * HD, (h + 1) * HD)
        scores = jnp.where(mask, dot(key[:, cols], query_ref[:, cols], NT), -big)
        top = jnp.max(scores, axis=0, keepdims=True)
        weights = jnp.exp(scores - top)
        total = jnp.sum(weights, axis=0, keepdims=True)
        summed = dot(value[:, cols], weights.astype(jnp.bfloat16), TN)
        sum_ref[cols, :] = summed / total
        log_ref[h : h + 1, :] = top + jnp.log(total)


def absorb(carry, found):
    top, total, summed = carry
    new_top = top
    for scores, mask, _ in found:
        best = jnp.max(scores, axis=0, keepdims=True)
        new_top = jnp.maximum(new_top, jnp.where(mask, best, -big))
    factor = jnp.exp(top - new_top)
    total, summed = total * factor, summed * factor
    for scores, mask, values in found:
        weights = jnp.exp(scores - jnp.where(mask, new_top, big))
        total = total + jnp.sum(weights, axis=0, keepdims=True)
        summed = summed + dot(values, weights.astype(jnp.bfloat16), TN)
    return new_top, total, summed


def questions(asks, rows, per):
    queries = [
        jnp.concatenate([ref[i * rows : (i + 1) * rows, :] for ref in asks], axis=0) for i in range(per)
    ]
    at = per * (rows + 2 * HD)
    notes = [ref[at : at + NOTE_ROWS, :].astype(jnp.float32)[1:2, :] for ref in asks]
    return queries, jnp.concatenate(notes, axis=1)


def block_scores(ref, at, queries, group):
    per = len(queries)
    tag = ref[pl.ds(at + 2 * HD * per, NOTE_ROWS), :].astype(jnp.float32)[0:1, 0:1]
    found = []
    for i, query in enumerate(queries):
        keys, values = (ref[pl.ds(at + j * HD, HD), :] for j in (2 * i, 2 * i + 1))
        found.append((dot(keys, query, NT), group == tag, values))
    return found


def first_kernel(rows, per, *refs):
    asks, fars, (state_ref, sum_ref) = refs[:2], refs[2:-2], refs[-2:]
    queries, group = questions(asks, rows, per)
    tokens = group.shape[1]
    found = [block_scores(ref, per * rows, queries, group) for ref in asks]
    step = 2 * HD * per + NOTE_ROWS
    for ref in fars:
        found += [block_scores(ref, at, queries, group) for at in range(0, ref.shape[0], step)]
    for i in range(per):
        carry = (
            jnp.full((1, tokens), -big, jnp.float32),
            jnp.zeros((1, tokens), jnp.float32),
            jnp.zeros((HD, tokens), jnp.float32),
        )
        top, total, summed = absorb(carry, [block[i] for block in found])
        cols = slice(i * tokens, (i + 1) * tokens)
        state_ref[0:1, cols] = top
        state_ref[1:2, cols] = total
        sum_ref[:, cols] = summed


def second_kernel(rows, per, *refs):
    asks, (state_ref, sum_ref), blocks, outs = refs[:2], refs[2:4], refs[4:-2], refs[-2:]
    queries, group = questions(asks, rows, per)
    tokens = group.shape[1]
    step = 2 * HD * per + NOTE_ROWS
    cols = [slice(i * tokens, (i + 1) * tokens) for i in range(per)]
    carry = [(state_ref[0:1, at], state_ref[1:2, at], sum_ref[:, at]) for at in cols]
    found = [
        block_scores(ref, at, queries, group)
        for ref in blocks
        if ref.shape[0] <= 2 * step
        for at in range(0, ref.shape[0], step)
    ]
    carry = tuple(absorb(carry[i], [block[i] for block in found]) for i in range(per))
    for ref in blocks:
        if ref.shape[0] > 2 * step:

            def body(b, state, ref=ref):
                block = block_scores(ref, pl.multiple_of(b * step, NOTE_ROWS), queries, group)
                return tuple(absorb(state[i], [block[i]]) for i in range(per))

            carry = lax.fori_loop(0, ref.shape[0] // step, body, carry)
    logs = [jnp.zeros((NOTE_ROWS, rows), jnp.float32)] * len(outs)
    place = lax.broadcasted_iota(jnp.int32, (NOTE_ROWS, rows), 0)
    for i, (top, total, summed) in enumerate(carry):
        found = total > 0.0
        summed = summed * jnp.where(found, 1.0 / jnp.where(found, total, 1.0), 0.0)
        log = jnp.where(found, top + jnp.log(jnp.where(found, total, 1.0)), -big)
        first = log.astype(jnp.bfloat16).astype(jnp.float32)
        second = (log - first).astype(jnp.bfloat16).astype(jnp.float32)
        for k, out in enumerate(outs):
            at = slice(k * rows, (k + 1) * rows)
            out[i * HD : (i + 1) * HD, :] = summed[:, at].astype(jnp.bfloat16)
            for j, term in enumerate((first, second, log - first - second)):
                logs[k] = jnp.where(place == 3 * i + j, term[:, at], logs[k])
    for k, out in enumerate(outs):
        out[per * HD : per * HD + NOTE_ROWS, :] = logs[k].astype(jnp.bfloat16)


def project_kernel(per, sum_ref, log_ref, w_out_ref, *refs):
    backs, (keep_ref, send_ref, attended, branch) = refs[:2], refs[2:]
    for bits, back in zip(ORDER, backs):
        logs = back[per * HD : per * HD + NOTE_ROWS, :].astype(jnp.float32)
        for i in range(per):
            at = head_at(bits, i, per)
            prefix_log = logs[3 * i : 3 * i + 1, :] + logs[3 * i + 1 : 3 * i + 2, :] + logs[3 * i + 2 : 3 * i + 3, :]
            suffix_log = log_ref[pl.ds(lax.div(at, HD), 1), :]
            top = jnp.maximum(prefix_log, suffix_log)
            prefix_part = jnp.exp(prefix_log - top)
            suffix_part = jnp.exp(suffix_log - top)
            whole = prefix_part + suffix_part
            joined = (
                back[i * HD : (i + 1) * HD, :].astype(jnp.float32) * (prefix_part / whole)
                + sum_ref[pl.ds(at, HD), :] * (suffix_part / whole)
            )
            attended[pl.ds(at, HD), :] = joined.astype(jnp.bfloat16)
    branch[...] = dot(attended[...], w_out_ref[...], TN)
    half = keep_ref.shape[0]
    side = lax.rem(lax.axis_index("mp"), 2)
    keep_ref[...] = branch[pl.ds(pl.multiple_of(side * half, half), half), :]
    other = branch[pl.ds(pl.multiple_of((1 - side) * half, half), half), :]
    send_ref[...] = other.astype(jnp.bfloat16)


def own_half_kernel(half_ref, out_ref, sem):
    half = half_ref.shape[0]
    side = lax.rem(lax.axis_index("mp"), 2)
    rows = pl.ds(pl.multiple_of(side * half, half), half)
    copy = pltpu.make_async_copy(half_ref, out_ref.at[rows, :], sem.at[0])
    copy.start()
    copy.wait()


def other_half_kernel(half_ref, _, out_ref, sem):
    half = half_ref.shape[0]
    side = lax.rem(lax.axis_index("mp"), 2)
    rows = pl.ds(pl.multiple_of((1 - side) * half, half), half)
    copy = pltpu.make_async_copy(half_ref, out_ref.at[rows, :], sem.at[0])
    copy.start()
    copy.wait()


def call(kernel, outs, specs, scratch=(), out_specs=None, aliases=None, cost=1):
    def run(*args):
        pinned = [
            pltpu.with_memory_space_constraint(x, pltpu.HBM) if spec is HBM else x
            for x, spec in zip(args, specs)
        ]
        return inner(*pinned)

    inner = pl.pallas_call(
        kernel,
        out_shape=tuple(jax.ShapeDtypeStruct(s, t) for s, t in outs),
        in_specs=specs,
        out_specs=out_specs or (VMEM,) * len(outs),
        scratch_shapes=scratch,
        input_output_aliases=aliases or {},
        compiler_params=pltpu.CompilerParams(vmem_limit_bytes=40 * 1024 * 1024),
        cost_estimate=pl.CostEstimate(flops=int(cost * 10**9), bytes_accessed=1, transcendentals=0),
    )
    return run


def local(
    hidden_in,
    norm_gain,
    norm_bias,
    w_query,
    w_key,
    w_value,
    w_out,
    prefix_keys,
    prefix_values,
    segment,
    request_group,
    block_slot,
    block_live,
):
    bf16, f32, i32 = jnp.bfloat16, jnp.float32, jnp.int32
    rows, width = hidden_in.shape
    local_width = w_query.shape[1]
    heads = local_width // HD
    n_blk = lax.axis_size("blk")
    n_mp = lax.axis_size("mp")
    per = heads // 2
    step = 2 * HD * per + NOTE_ROWS
    side = lax.rem(lax.axis_index("mp"), 2)

    def exchange(x, bits, far=0, back=False):
        pairs = []
        for i in range(n_blk):
            square, pair, lane = i // 4, i // 2 % 2, i % 2
            for m in range(n_mp):
                other, core = m // 2, m % 2
                blk = (square ^ far) * 4 + (pair ^ bits) * 2 + core
                link = (i * n_mp + m, blk * n_mp + other * 2 + 1 - lane)
                pairs.append(link[::-1] if back else link)
        return lax.ppermute(x, ("blk", "mp"), pairs)

    def across(x, bit):
        return lax.ppermute(x, "blk", [(i, i ^ bit) for i in range(n_blk)])

    def across_mp(x, bit):
        return lax.ppermute(x, "mp", [(i, i ^ bit) for i in range(n_mp)])

    group = jnp.where(block_live == 1, block_slot * GROUPS // n_blk, -1).astype(bf16)
    tag = jnp.broadcast_to(group, (NOTE_ROWS, HD))
    fars = []
    if n_blk == 8:
        fars = call(
            functools.partial(far_kernel, per),
            [((step, HD), bf16)] * 2,
            (HBM, HBM, VMEM),
            [pltpu.SemaphoreType.DMA((4 * per,))],
        )(prefix_keys, prefix_values, tag)
        fars = [exchange(fars[k], k, far=1) for k in ORDER]
    normed, query, *packs = call(
        functools.partial(query_kernel, per),
        [((rows, width), bf16), ((rows, local_width), bf16)]
        + [((per * rows + step, HD), bf16)] * 2,
        (HBM, HBM, VMEM) + (HBM,) * 6,
        [
            pltpu.VMEM((rows, width), bf16),
            pltpu.VMEM(w_query.shape, bf16),
            pltpu.VMEM((1, width), f32),
            pltpu.VMEM((1, width), f32),
            pltpu.VMEM(segment.shape, i32),
            pltpu.SMEM(request_group.shape, i32),
            pltpu.SemaphoreType.DMA((4 + ROW_CUTS + W_CUTS + 2 * heads,)),
        ],
        cost=Q,
    )(
        prefix_keys,
        prefix_values,
        tag,
        hidden_in,
        w_query,
        norm_gain.reshape(1, width),
        norm_bias.reshape(1, width),
        segment,
        request_group,
    )
    asks = [exchange(packs[k], k) for k in ORDER]
    suffix_sum, suffix_log = call(
        functools.partial(suffix_kernel, heads),
        [((local_width, rows), f32), ((max(heads, 8), rows), f32)],
        (VMEM,) * 2 + (HBM,) * 3,
        [
            pltpu.VMEM(segment.shape, i32),
            pltpu.VMEM(w_key.shape, bf16),
            pltpu.VMEM(w_value.shape, bf16),
            pltpu.SemaphoreType.DMA((1 + 2 * W_CUTS,)),
        ],
        cost=SFX,
    )(normed, query, segment, w_key, w_value)
    if fars:
        fars = list(call(join_kernel, [((2 * step, HD), bf16)], (VMEM,) * 3, cost=JOIN)(suffix_log, *fars))

    blocks = [x[per * rows :] for x in asks] + fars
    state, summed = call(
        functools.partial(first_kernel, rows, per),
        [((8, heads * rows), f32), ((HD, heads * rows), f32)],
        (VMEM,) * (2 + len(fars)),
    )(*asks, *fars)
    others = [across_mp(x, 1) for x in blocks]
    bit = 4
    while bit < n_blk and not fars:
        others = others + [across(jnp.concatenate(blocks + others, axis=0), bit)]
        bit *= 2
    backs = call(
        functools.partial(second_kernel, rows, per),
        [((per * HD + NOTE_ROWS, rows), bf16)] * 2,
        (VMEM,) * (4 + len(others)),
    )(*asks, state, summed, *others)
    backs = [exchange(x, k, back=True) for k, x in zip(ORDER, backs)]

    keep, send = call(
        functools.partial(project_kernel, per),
        [((rows // 2, width), f32), ((rows // 2, width), bf16)],
        (VMEM,) * 5,
        [pltpu.VMEM((local_width, rows), bf16), pltpu.VMEM((rows, width), f32)],
    )(suffix_sum, suffix_log, w_out, *backs)

    mine = (keep + across_mp(send, 1).astype(f32)).astype(bf16)
    bit = 2
    while bit < n_mp:
        mine = (mine.astype(f32) + across_mp(mine, bit).astype(f32)).astype(bf16 if 2 * bit < n_mp else f32)
        bit *= 2
    inputs = lax.dynamic_slice_in_dim(hidden_in, side * (rows // 2), rows // 2, 0)
    done = (inputs.astype(f32) + mine.astype(f32)).astype(bf16)
    other = across_mp(done, 1)
    whole = call(
        own_half_kernel,
        [((rows, width), bf16)],
        (VMEM,),
        [pltpu.SemaphoreType.DMA((1,))],
        (HBM,),
    )(done)[0]
    return call(
        other_half_kernel,
        [((rows, width), bf16)],
        (VMEM, HBM),
        [pltpu.SemaphoreType.DMA((1,))],
        (HBM,),
        {1: 0},
    )(other, whole)[0]


def solution(mesh):
    return jax.shard_map(
        local,
        mesh=mesh,
        in_specs=(
            P("blk", None),
            P(),
            P(),
            P(None, "mp"),
            P(None, "mp"),
            P(None, "mp"),
            P("mp", None),
            P("blk", None, "mp"),
            P("blk", None, "mp"),
            P("blk", None),
            P("blk", None),
            P("blk"),
            P("blk"),
        ),
        out_specs=P("blk", None),
        check_vma=False,
    )
```

```python
import functools

import jax
import jax.numpy as jnp
from jax import lax
from jax.experimental import pallas as pl
from jax.experimental.pallas import tpu as pltpu
from jax.sharding import PartitionSpec as P

HD = 128
GROUPS = 4
NOTE_ROWS = 16
ASK_ROWS = NOTE_ROWS + 128
W_CUTS = 4
ROW_CUTS = 2

ORDER = (1, 0)

big = 1e30
Q = 3
SFX = 10
JOIN = 30

VMEM = pl.BlockSpec(memory_space=pltpu.VMEM)
HBM = pl.BlockSpec(memory_space=pltpu.HBM)
NT = (((1,), (1,)), ((), ()))
TN = (((0,), (0,)), ((), ()))


def dot(a, b, dims=(((1,), (0,)), ((), ()))):
    return lax.dot_general(a, b, dims, preferred_element_type=jnp.float32)


def head_at(bits, i, per):
    pair = lax.rem(lax.div(lax.axis_index("blk"), 2), 2)
    return pl.multiple_of(((pair ^ bits) * per + i) * HD, HD)


def start_all(pairs, sems):
    copies = [pltpu.make_async_copy(a, b, sems.at[i]) for i, (a, b) in enumerate(pairs)]
    for copy in copies:
        copy.start()
    return copies


def block_copies(per, bits, keys_ref, values_ref, out, at):
    pairs = []
    for i in range(per):
        cols = pl.ds(head_at(bits, i, per), HD)
        pairs.append((keys_ref.at[0, :, cols], out.at[at : at + HD, :]))
        pairs.append((values_ref.at[0, :, cols], out.at[at + HD : at + 2 * HD, :]))
        at += 2 * HD
    return pairs


def pack_kernel(per, keys_ref, values_ref, tag_ref, *refs):
    outs, sems = refs[:-1], refs[-1]
    pairs = []
    for bits, out in zip((1, 0, 1), outs):
        pairs += block_copies(per, bits, keys_ref, values_ref, out, 0)
    copies = start_all(pairs, sems)
    for out in outs:
        out[2 * HD * per : 2 * HD * per + NOTE_ROWS, :] = tag_ref[...]
    for copy in copies:
        copy.wait()


def join_kernel(_, *refs):
    out = refs[-1]
    for i, ref in enumerate(refs[:-1]):
        out[i * ref.shape[0] : (i + 1) * ref.shape[0], :] = ref[...]


def query_kernel(per, *refs):
    keys_ref, values_ref, tag_ref, hidden_in, w_query, *sources = refs[:9]
    normed_ref, query_ref = refs[9:11]
    outs, held, sems = refs[11:13], refs[13:-1], refs[-1]
    hidden_ref, w_query_ref, gain_ref, bias_ref, segment_ref, request_group_ref = held
    rows, width = hidden_ref.shape
    row_cuts = [pl.ds(i * (rows // ROW_CUTS), rows // ROW_CUTS) for i in range(ROW_CUTS)]
    w_cuts = [pl.ds(i * (width // W_CUTS), width // W_CUTS) for i in range(W_CUTS)]
    pairs = [(hidden_in.at[cut, :], hidden_ref.at[cut, :]) for cut in row_cuts]
    pairs += list(zip(sources, held[2:]))
    pairs += [(w_query.at[cut, :], w_query_ref.at[cut, :]) for cut in w_cuts]
    pairs += block_copies(per, 0, keys_ref, values_ref, outs[0], per * rows)
    copies = start_all(pairs, sems)
    small = copies[ROW_CUTS : ROW_CUTS + 4]
    weights = copies[ROW_CUTS + 4 : ROW_CUTS + 4 + W_CUTS]
    for cut, copy in zip(row_cuts, copies):
        copy.wait()
        if cut is row_cuts[0]:
            small[0].wait()
            small[1].wait()
        inputs = hidden_ref[cut, :].astype(jnp.float32)
        mean = jnp.mean(inputs, axis=-1, keepdims=True)
        centred = inputs - mean
        var = jnp.mean(centred * centred, axis=-1, keepdims=True)
        normed = centred * lax.rsqrt(var + 1e-05) * gain_ref[...] + bias_ref[...]
        normed_ref[cut, :] = normed.astype(jnp.bfloat16)
    small[2].wait()
    small[3].wait()
    segment = segment_ref[...]
    group = jnp.zeros_like(segment)
    for r in range(request_group_ref.shape[1]):
        group = jnp.where(segment == r, request_group_ref[0, r], group)
    tag = tag_ref[...].astype(jnp.float32)
    place = lax.broadcasted_iota(jnp.int32, tag.shape, 0)
    notes = jnp.where(place == 0, tag, group.astype(jnp.float32)).astype(jnp.bfloat16)
    query = jnp.zeros(query_ref.shape, jnp.float32)
    for cut, copy in zip(w_cuts, weights):
        copy.wait()
        query = query + dot(normed_ref[:, cut], w_query_ref[cut, :])
    query_ref[...] = (query * (HD**-0.5)).astype(jnp.bfloat16)
    for bits, out in enumerate(outs):
        for i in range(per):
            out[i * rows : (i + 1) * rows, :] = query_ref[:, pl.ds(head_at(bits, i, per), HD)]
        out[out.shape[0] - NOTE_ROWS : out.shape[0], :] = notes
    for copy in copies[ROW_CUTS + 4 + W_CUTS :]:
        copy.wait()


def suffix_kernel(heads, normed_ref, query_ref, *refs):
    sources, (sum_ref, log_ref), held, sems = refs[:3], refs[3:5], refs[5:8], refs[8]
    segment_ref, w_key_ref, w_value_ref = held
    rows, width = normed_ref.shape
    cut = width // W_CUTS
    pairs = [(sources[0], held[0])]
    for source, target in zip(sources[1:], held[1:]):
        parts = [pl.ds(i * cut, cut) for i in range(W_CUTS)]
        pairs += [(source.at[part, :], target.at[part, :]) for part in parts]
    copies = start_all(pairs, sems)

    def project(target, waits):
        out = jnp.zeros((rows, target.shape[1]), jnp.float32)
        for i, copy in enumerate(waits):
            copy.wait()
            at = slice(i * cut, (i + 1) * cut)
            out = out + dot(normed_ref[:, at], target[at, :])
        return out.astype(jnp.bfloat16)

    key = project(w_key_ref, copies[1 : 1 + W_CUTS])
    value = project(w_value_ref, copies[1 + W_CUTS :])
    copies[0].wait()
    by_token = jnp.broadcast_to(segment_ref[...], (rows, rows))
    key_place = lax.broadcasted_iota(jnp.int32, (rows, rows), 0)
    token_place = lax.broadcasted_iota(jnp.int32, (rows, rows), 1)
    by_key = jnp.sum(
        jnp.where(key_place == token_place, by_token, 0).astype(jnp.float32), axis=1, keepdims=True
    )
    mask = (by_key == by_token.astype(jnp.float32)) & (key_place <= token_place)
    for h in range(heads):
        cols = slice(h * HD, (h + 1) * HD)
        scores = jnp.where(mask, dot(key[:, cols], query_ref[:, cols], NT), -big)
        top = jnp.max(scores, axis=0, keepdims=True)
        weights = jnp.exp(scores - top)
        total = jnp.sum(weights, axis=0, keepdims=True)
        summed = dot(value[:, cols], weights.astype(jnp.bfloat16), TN)
        sum_ref[cols, :] = summed / total
        log_ref[h : h + 1, :] = top + jnp.log(total)


def absorb(carry, found):
    top, total, summed = carry
    new_top = top
    for scores, mask, _ in found:
        best = jnp.max(scores, axis=0, keepdims=True)
        new_top = jnp.maximum(new_top, jnp.where(mask, best, -big))
    factor = jnp.exp(top - new_top)
    total, summed = total * factor, summed * factor
    for scores, mask, values in found:
        weights = jnp.exp(scores - jnp.where(mask, new_top, big))
        total = total + jnp.sum(weights, axis=0, keepdims=True)
        summed = summed + dot(values, weights.astype(jnp.bfloat16), TN)
    return new_top, total, summed


def questions(asks, rows, per):
    queries = [
        jnp.concatenate([ref[i * rows : (i + 1) * rows, :] for ref in asks], axis=0) for i in range(per)
    ]
    notes = [ref[ref.shape[0] - NOTE_ROWS : ref.shape[0], :].astype(jnp.float32)[1:2, :] for ref in asks]
    return queries, jnp.concatenate(notes, axis=1)


def block_scores(ref, at, queries, group):
    per = len(queries)
    tag = ref[pl.ds(at + 2 * HD * per, NOTE_ROWS), :].astype(jnp.float32)[0:1, 0:1]
    found = []
    for i, query in enumerate(queries):
        keys, values = (ref[pl.ds(at + j * HD, HD), :] for j in (2 * i, 2 * i + 1))
        found.append((dot(keys, query, NT), group == tag, values))
    return found


def first_kernel(rows, per, *refs):
    asks, early, (state_ref, sum_ref) = refs[:2], refs[2], refs[3:]
    queries, group = questions(asks, rows, per)
    tokens = group.shape[1]
    step = 2 * HD * per + NOTE_ROWS
    found = [block_scores(asks[1], per * rows, queries, group)]
    found += [block_scores(early, at, queries, group) for at in range(0, early.shape[0], step)]
    for i in range(per):
        carry = (
            jnp.full((1, tokens), -big, jnp.float32),
            jnp.zeros((1, tokens), jnp.float32),
            jnp.zeros((HD, tokens), jnp.float32),
        )
        top, total, summed = absorb(carry, [block[i] for block in found])
        cols = slice(i * tokens, (i + 1) * tokens)
        state_ref[0:1, cols] = top
        state_ref[1:2, cols] = total
        sum_ref[:, cols] = summed


def second_kernel(rows, per, *refs):
    asks, (state_ref, sum_ref), blocks, outs = refs[:2], refs[2:4], refs[4:-2], refs[-2:]
    queries, group = questions(asks, rows, per)
    tokens = group.shape[1]
    step = 2 * HD * per + NOTE_ROWS
    cols = [slice(i * tokens, (i + 1) * tokens) for i in range(per)]
    carry = [(state_ref[0:1, at], state_ref[1:2, at], sum_ref[:, at]) for at in cols]
    found = [
        block_scores(ref, at, queries, group)
        for ref in blocks
        if ref.shape[0] <= 3 * step
        for at in range(0, ref.shape[0], step)
    ]
    carry = tuple(absorb(carry[i], [block[i] for block in found]) for i in range(per))
    for ref in blocks:
        if ref.shape[0] > 3 * step:

            def body(b, state, ref=ref):
                block = block_scores(ref, pl.multiple_of(b * step, NOTE_ROWS), queries, group)
                return tuple(absorb(state[i], [block[i]]) for i in range(per))

            carry = lax.fori_loop(0, ref.shape[0] // step, body, carry)
    logs = [jnp.zeros((NOTE_ROWS, rows), jnp.float32)] * len(outs)
    place = lax.broadcasted_iota(jnp.int32, (NOTE_ROWS, rows), 0)
    for i, (top, total, summed) in enumerate(carry):
        found = total > 0.0
        summed = summed * jnp.where(found, 1.0 / jnp.where(found, total, 1.0), 0.0)
        log = jnp.where(found, top + jnp.log(jnp.where(found, total, 1.0)), -big)
        first = log.astype(jnp.bfloat16).astype(jnp.float32)
        second = (log - first).astype(jnp.bfloat16).astype(jnp.float32)
        for k, out in enumerate(outs):
            at = slice(k * rows, (k + 1) * rows)
            out[i * HD : (i + 1) * HD, :] = summed[:, at].astype(jnp.bfloat16)
            for j, term in enumerate((first, second, log - first - second)):
                logs[k] = jnp.where(place == 3 * i + j, term[:, at], logs[k])
    for k, out in enumerate(outs):
        out[per * HD : per * HD + NOTE_ROWS, :] = logs[k].astype(jnp.bfloat16)


def project_kernel(per, sum_ref, log_ref, w_out_ref, *refs):
    backs, (keep_ref, send_ref, attended, branch) = refs[:2], refs[2:]
    for bits, back in zip(ORDER, backs):
        logs = back[per * HD : per * HD + NOTE_ROWS, :].astype(jnp.float32)
        for i in range(per):
            at = head_at(bits, i, per)
            prefix_log = logs[3 * i : 3 * i + 1, :] + logs[3 * i + 1 : 3 * i + 2, :] + logs[3 * i + 2 : 3 * i + 3, :]
            suffix_log = log_ref[pl.ds(lax.div(at, HD), 1), :]
            top = jnp.maximum(prefix_log, suffix_log)
            prefix_part = jnp.exp(prefix_log - top)
            suffix_part = jnp.exp(suffix_log - top)
            whole = prefix_part + suffix_part
            joined = (
                back[i * HD : (i + 1) * HD, :].astype(jnp.float32) * (prefix_part / whole)
                + sum_ref[pl.ds(at, HD), :] * (suffix_part / whole)
            )
            attended[pl.ds(at, HD), :] = joined.astype(jnp.bfloat16)
    branch[...] = dot(attended[...], w_out_ref[...], TN)
    half = keep_ref.shape[0]
    side = lax.rem(lax.axis_index("mp"), 2)
    keep_ref[...] = branch[pl.ds(pl.multiple_of(side * half, half), half), :]
    other = branch[pl.ds(pl.multiple_of((1 - side) * half, half), half), :]
    send_ref[...] = other.astype(jnp.bfloat16)


def own_half_kernel(half_ref, out_ref, sem):
    half = half_ref.shape[0]
    side = lax.rem(lax.axis_index("mp"), 2)
    rows = pl.ds(pl.multiple_of(side * half, half), half)
    copy = pltpu.make_async_copy(half_ref, out_ref.at[rows, :], sem.at[0])
    copy.start()
    copy.wait()


def other_half_kernel(half_ref, _, out_ref, sem):
    half = half_ref.shape[0]
    side = lax.rem(lax.axis_index("mp"), 2)
    rows = pl.ds(pl.multiple_of((1 - side) * half, half), half)
    copy = pltpu.make_async_copy(half_ref, out_ref.at[rows, :], sem.at[0])
    copy.start()
    copy.wait()


def call(kernel, outs, specs, scratch=(), out_specs=None, aliases=None, cost=1):
    def run(*args):
        pinned = [
            pltpu.with_memory_space_constraint(x, pltpu.HBM) if spec is HBM else x
            for x, spec in zip(args, specs)
        ]
        return inner(*pinned)

    inner = pl.pallas_call(
        kernel,
        out_shape=tuple(jax.ShapeDtypeStruct(s, t) for s, t in outs),
        in_specs=specs,
        out_specs=out_specs or (VMEM,) * len(outs),
        scratch_shapes=scratch,
        input_output_aliases=aliases or {},
        compiler_params=pltpu.CompilerParams(vmem_limit_bytes=40 * 1024 * 1024),
        cost_estimate=pl.CostEstimate(flops=int(cost * 10**9), bytes_accessed=1, transcendentals=0),
    )
    return run


def local(
    hidden_in,
    norm_gain,
    norm_bias,
    w_query,
    w_key,
    w_value,
    w_out,
    prefix_keys,
    prefix_values,
    segment,
    request_group,
    block_slot,
    block_live,
):
    bf16, f32, i32 = jnp.bfloat16, jnp.float32, jnp.int32
    rows, width = hidden_in.shape
    local_width = w_query.shape[1]
    heads = local_width // HD
    n_blk = lax.axis_size("blk")
    n_mp = lax.axis_size("mp")
    per = heads // 2
    step = 2 * HD * per + NOTE_ROWS
    side = lax.rem(lax.axis_index("mp"), 2)

    def exchange(x, bits, far=0, back=False):
        pairs = []
        for i in range(n_blk):
            square, pair, lane = i // 4, i // 2 % 2, i % 2
            for m in range(n_mp):
                other, core = m // 2, m % 2
                blk = (square ^ far) * 4 + (pair ^ bits) * 2 + core
                link = (i * n_mp + m, blk * n_mp + other * 2 + 1 - lane)
                pairs.append(link[::-1] if back else link)
        return lax.ppermute(x, ("blk", "mp"), pairs)

    def across(x, bit):
        return lax.ppermute(x, "blk", [(i, i ^ bit) for i in range(n_blk)])

    def across_mp(x, bit):
        return lax.ppermute(x, "mp", [(i, i ^ bit) for i in range(n_mp)])

    group = jnp.where(block_live == 1, block_slot * GROUPS // n_blk, -1).astype(bf16)
    tag = jnp.broadcast_to(group, (NOTE_ROWS, HD))
    early = call(
        functools.partial(pack_kernel, per),
        [((step, HD), bf16)] * (3 if n_blk == 8 else 1),
        (HBM, HBM, VMEM),
        [pltpu.SemaphoreType.DMA(((6 if n_blk == 8 else 2) * per,))],
    )(prefix_keys, prefix_values, tag)
    near = exchange(early[0], 1)
    fars = [exchange(early[1 + k], k, far=1) for k in (0, 1)] if n_blk == 8 else []
    normed, query, *packs = call(
        functools.partial(query_kernel, per),
        [((rows, width), bf16), ((rows, local_width), bf16)]
        + [((per * rows + n, HD), bf16) for n in (step, NOTE_ROWS)],
        (HBM, HBM, VMEM) + (HBM,) * 6,
        [
            pltpu.VMEM((rows, width), bf16),
            pltpu.VMEM(w_query.shape, bf16),
            pltpu.VMEM((1, width), f32),
            pltpu.VMEM((1, width), f32),
            pltpu.VMEM(segment.shape, i32),
            pltpu.SMEM(request_group.shape, i32),
            pltpu.SemaphoreType.DMA((4 + ROW_CUTS + W_CUTS + 2 * per,)),
        ],
        cost=Q,
    )(
        prefix_keys,
        prefix_values,
        tag,
        hidden_in,
        w_query,
        norm_gain.reshape(1, width),
        norm_bias.reshape(1, width),
        segment,
        request_group,
    )
    asks = [exchange(packs[k], k) for k in ORDER]
    suffix_sum, suffix_log = call(
        functools.partial(suffix_kernel, heads),
        [((local_width, rows), f32), ((max(heads, 8), rows), f32)],
        (VMEM,) * 2 + (HBM,) * 3,
        [
            pltpu.VMEM(segment.shape, i32),
            pltpu.VMEM(w_key.shape, bf16),
            pltpu.VMEM(w_value.shape, bf16),
            pltpu.SemaphoreType.DMA((1 + 2 * W_CUTS,)),
        ],
        cost=SFX,
    )(normed, query, segment, w_key, w_value)
    joined = near
    if fars:
        join = call(join_kernel, [((3 * step, HD), bf16)], (VMEM,) * 4, cost=JOIN)
        joined = join(suffix_log, fars[0], near, fars[1])[0]

    blocks = [joined, asks[1][per * rows :]]
    state, summed = call(
        functools.partial(first_kernel, rows, per),
        [((8, heads * rows), f32), ((HD, heads * rows), f32)],
        (VMEM,) * 3,
        cost=30,
    )(*asks, joined)
    others = [across_mp(x, 1) for x in blocks]
    bit = 4
    while bit < n_blk and not fars:
        others = others + [across(jnp.concatenate(blocks + others, axis=0), bit)]
        bit *= 2
    backs = call(
        functools.partial(second_kernel, rows, per),
        [((per * HD + NOTE_ROWS, rows), bf16)] * 2,
        (VMEM,) * (4 + len(others)),
    )(*asks, state, summed, *others)
    backs = [exchange(x, k, back=True) for k, x in zip(ORDER, backs)]

    keep, send = call(
        functools.partial(project_kernel, per),
        [((rows // 2, width), f32), ((rows // 2, width), bf16)],
        (VMEM,) * 5,
        [pltpu.VMEM((local_width, rows), bf16), pltpu.VMEM((rows, width), f32)],
    )(suffix_sum, suffix_log, w_out, *backs)

    mine = (keep + across_mp(send, 1).astype(f32)).astype(bf16)
    bit = 2
    while bit < n_mp:
        mine = (mine.astype(f32) + across_mp(mine, bit).astype(f32)).astype(bf16 if 2 * bit < n_mp else f32)
        bit *= 2
    inputs = lax.dynamic_slice_in_dim(hidden_in, side * (rows // 2), rows // 2, 0)
    done = (inputs.astype(f32) + mine.astype(f32)).astype(bf16)
    other = across_mp(done, 1)
    whole = call(
        own_half_kernel,
        [((rows, width), bf16)],
        (VMEM,),
        [pltpu.SemaphoreType.DMA((1,))],
        (HBM,),
    )(done)[0]
    return call(
        other_half_kernel,
        [((rows, width), bf16)],
        (VMEM, HBM),
        [pltpu.SemaphoreType.DMA((1,))],
        (HBM,),
        {1: 0},
    )(other, whole)[0]


def solution(mesh):
    return jax.shard_map(
        local,
        mesh=mesh,
        in_specs=(
            P("blk", None),
            P(),
            P(),
            P(None, "mp"),
            P(None, "mp"),
            P(None, "mp"),
            P("mp", None),
            P("blk", None, "mp"),
            P("blk", None, "mp"),
            P("blk", None),
            P("blk", None),
            P("blk"),
            P("blk"),
        ),
        out_specs=P("blk", None),
        check_vma=False,
    )
```

```python
import functools

import jax
import jax.numpy as jnp
from jax import lax
from jax.experimental import pallas as pl
from jax.experimental.pallas import tpu as pltpu
from jax.sharding import PartitionSpec as P

HD = 128
GROUPS = 4
NOTE_ROWS = 16
ASK_ROWS = NOTE_ROWS + 128
W_CUTS = 4
ROW_CUTS = 2

ORDER = (1, 0)
BACK = (0, 1)

big = 1e30
Q = 0.001
SFX = 0.001
JOIN = 30
JOIN1 = 0.001

VMEM = pl.BlockSpec(memory_space=pltpu.VMEM)
HBM = pl.BlockSpec(memory_space=pltpu.HBM)
NT = (((1,), (1,)), ((), ()))
TN = (((0,), (0,)), ((), ()))


def dot(a, b, dims=(((1,), (0,)), ((), ()))):
    return lax.dot_general(a, b, dims, preferred_element_type=jnp.float32)


def head_at(bits, i, per):
    pair = lax.rem(lax.div(lax.axis_index("blk"), 2), 2)
    return pl.multiple_of(((pair ^ bits) * per + i) * HD, HD)


def start_all(pairs, sems):
    copies = [pltpu.make_async_copy(a, b, sems.at[i]) for i, (a, b) in enumerate(pairs)]
    for copy in copies:
        copy.start()
    return copies


def block_copies(per, bits, keys_ref, values_ref, out, at):
    pairs = []
    for i in range(per):
        cols = pl.ds(head_at(bits, i, per), HD)
        pairs.append((keys_ref.at[0, :, cols], out.at[at : at + HD, :]))
        pairs.append((values_ref.at[0, :, cols], out.at[at + HD : at + 2 * HD, :]))
        at += 2 * HD
    return pairs


def pack_kernel(per, keys_ref, values_ref, tag_ref, *refs):
    outs, sems = refs[:-1], refs[-1]
    pairs = []
    for bits, out in zip((1, 0, 1), outs):
        pairs += block_copies(per, bits, keys_ref, values_ref, out, 0)
    copies = start_all(pairs, sems)
    for out in outs:
        out[2 * HD * per : 2 * HD * per + NOTE_ROWS, :] = tag_ref[...]
    for copy in copies:
        copy.wait()


def join_kernel(_, *refs):
    out = refs[-1]
    for i, ref in enumerate(refs[:-1]):
        out[i * ref.shape[0] : (i + 1) * ref.shape[0], :] = ref[...]


def query_kernel(per, *refs):
    keys_ref, values_ref, tag_ref, hidden_in, w_query, *sources = refs[:9]
    normed_ref, query_ref = refs[9:11]
    outs, held, sems = refs[11:13], refs[13:-1], refs[-1]
    hidden_ref, w_query_ref, gain_ref, bias_ref, segment_ref, request_group_ref = held
    rows, width = hidden_ref.shape
    row_cuts = [pl.ds(i * (rows // ROW_CUTS), rows // ROW_CUTS) for i in range(ROW_CUTS)]
    w_cuts = [pl.ds(i * (width // W_CUTS), width // W_CUTS) for i in range(W_CUTS)]
    pairs = [(hidden_in.at[cut, :], hidden_ref.at[cut, :]) for cut in row_cuts]
    pairs += list(zip(sources, held[2:]))
    pairs += [(w_query.at[cut, :], w_query_ref.at[cut, :]) for cut in w_cuts]
    pairs += block_copies(per, 0, keys_ref, values_ref, outs[0], per * rows)
    copies = start_all(pairs, sems)
    small = copies[ROW_CUTS : ROW_CUTS + 4]
    weights = copies[ROW_CUTS + 4 : ROW_CUTS + 4 + W_CUTS]
    for cut, copy in zip(row_cuts, copies):
        copy.wait()
        if cut is row_cuts[0]:
            small[0].wait()
            small[1].wait()
        inputs = hidden_ref[cut, :].astype(jnp.float32)
        mean = jnp.mean(inputs, axis=-1, keepdims=True)
        centred = inputs - mean
        var = jnp.mean(centred * centred, axis=-1, keepdims=True)
        normed = centred * lax.rsqrt(var + 1e-05) * gain_ref[...] + bias_ref[...]
        normed_ref[cut, :] = normed.astype(jnp.bfloat16)
    small[2].wait()
    small[3].wait()
    segment = segment_ref[...]
    group = jnp.zeros_like(segment)
    for r in range(request_group_ref.shape[1]):
        group = jnp.where(segment == r, request_group_ref[0, r], group)
    tag = tag_ref[...].astype(jnp.float32)
    place = lax.broadcasted_iota(jnp.int32, tag.shape, 0)
    notes = jnp.where(place == 0, tag, group.astype(jnp.float32)).astype(jnp.bfloat16)
    query = jnp.zeros(query_ref.shape, jnp.float32)
    for cut, copy in zip(w_cuts, weights):
        copy.wait()
        query = query + dot(normed_ref[:, cut], w_query_ref[cut, :])
    query_ref[...] = (query * (HD**-0.5)).astype(jnp.bfloat16)
    for bits, out in enumerate(outs):
        for i in range(per):
            out[i * rows : (i + 1) * rows, :] = query_ref[:, pl.ds(head_at(bits, i, per), HD)]
        out[out.shape[0] - NOTE_ROWS : out.shape[0], :] = notes
    for copy in copies[ROW_CUTS + 4 + W_CUTS :]:
        copy.wait()


def suffix_kernel(heads, normed_ref, query_ref, *refs):
    sources, (sum_ref, log_ref), held, sems = refs[:3], refs[3:5], refs[5:8], refs[8]
    segment_ref, w_key_ref, w_value_ref = held
    rows, width = normed_ref.shape
    cut = width // W_CUTS
    pairs = [(sources[0], held[0])]
    for source, target in zip(sources[1:], held[1:]):
        parts = [pl.ds(i * cut, cut) for i in range(W_CUTS)]
        pairs += [(source.at[part, :], target.at[part, :]) for part in parts]
    copies = start_all(pairs, sems)

    def project(target, waits):
        out = jnp.zeros((rows, target.shape[1]), jnp.float32)
        for i, copy in enumerate(waits):
            copy.wait()
            at = slice(i * cut, (i + 1) * cut)
            out = out + dot(normed_ref[:, at], target[at, :])
        return out.astype(jnp.bfloat16)

    key = project(w_key_ref, copies[1 : 1 + W_CUTS])
    value = project(w_value_ref, copies[1 + W_CUTS :])
    copies[0].wait()
    by_token = jnp.broadcast_to(segment_ref[...], (rows, rows))
    key_place = lax.broadcasted_iota(jnp.int32, (rows, rows), 0)
    token_place = lax.broadcasted_iota(jnp.int32, (rows, rows), 1)
    by_key = jnp.sum(
        jnp.where(key_place == token_place, by_token, 0).astype(jnp.float32), axis=1, keepdims=True
    )
    mask = (by_key == by_token.astype(jnp.float32)) & (key_place <= token_place)
    for h in range(heads):
        cols = slice(h * HD, (h + 1) * HD)
        scores = jnp.where(mask, dot(key[:, cols], query_ref[:, cols], NT), -big)
        top = jnp.max(scores, axis=0, keepdims=True)
        weights = jnp.exp(scores - top)
        total = jnp.sum(weights, axis=0, keepdims=True)
        summed = dot(value[:, cols], weights.astype(jnp.bfloat16), TN)
        sum_ref[cols, :] = summed / total
        log_ref[h : h + 1, :] = top + jnp.log(total)


def absorb(carry, found):
    top, total, summed = carry
    new_top = top
    for scores, mask, _ in found:
        best = jnp.max(scores, axis=0, keepdims=True)
        new_top = jnp.maximum(new_top, jnp.where(mask, best, -big))
    factor = jnp.exp(top - new_top)
    total, summed = total * factor, summed * factor
    for scores, mask, values in found:
        weights = jnp.exp(scores - jnp.where(mask, new_top, big))
        total = total + jnp.sum(weights, axis=0, keepdims=True)
        summed = summed + dot(values, weights.astype(jnp.bfloat16), TN)
    return new_top, total, summed


def questions(asks, rows, per):
    queries = [
        jnp.concatenate([ref[i * rows : (i + 1) * rows, :] for ref in asks], axis=0) for i in range(per)
    ]
    notes = [ref[ref.shape[0] - NOTE_ROWS : ref.shape[0], :].astype(jnp.float32)[1:2, :] for ref in asks]
    return queries, jnp.concatenate(notes, axis=1)


def block_scores(ref, at, queries, group):
    per = len(queries)
    tag = ref[pl.ds(at + 2 * HD * per, NOTE_ROWS), :].astype(jnp.float32)[0:1, 0:1]
    found = []
    for i, query in enumerate(queries):
        keys, values = (ref[pl.ds(at + j * HD, HD), :] for j in (2 * i, 2 * i + 1))
        found.append((dot(keys, query, NT), group == tag, values))
    return found


def first_kernel(rows, per, *refs):
    asks, early, (state_ref, sum_ref) = refs[:2], refs[2:-2], refs[-2:]
    queries, group = questions(asks, rows, per)
    tokens = group.shape[1]
    step = 2 * HD * per + NOTE_ROWS
    found = [block_scores(asks[1], per * rows, queries, group)]
    for ref in early:
        found += [block_scores(ref, at, queries, group) for at in range(0, ref.shape[0], step)]
    for i in range(per):
        carry = (
            jnp.full((1, tokens), -big, jnp.float32),
            jnp.zeros((1, tokens), jnp.float32),
            jnp.zeros((HD, tokens), jnp.float32),
        )
        top, total, summed = absorb(carry, [block[i] for block in found])
        cols = slice(i * tokens, (i + 1) * tokens)
        state_ref[0:1, cols] = top
        state_ref[1:2, cols] = total
        sum_ref[:, cols] = summed


def second_kernel(rows, per, *refs):
    asks, (state_ref, sum_ref), blocks, outs = refs[:2], refs[2:4], refs[4:-2], refs[-2:]
    queries, group = questions(asks, rows, per)
    tokens = group.shape[1]
    step = 2 * HD * per + NOTE_ROWS
    cols = [slice(i * tokens, (i + 1) * tokens) for i in range(per)]
    carry = [(state_ref[0:1, at], state_ref[1:2, at], sum_ref[:, at]) for at in cols]
    found = [
        block_scores(ref, at, queries, group)
        for ref in blocks
        if ref.shape[0] <= 3 * step
        for at in range(0, ref.shape[0], step)
    ]
    carry = tuple(absorb(carry[i], [block[i] for block in found]) for i in range(per))
    for ref in blocks:
        if ref.shape[0] > 3 * step:

            def body(b, state, ref=ref):
                block = block_scores(ref, pl.multiple_of(b * step, NOTE_ROWS), queries, group)
                return tuple(absorb(state[i], [block[i]]) for i in range(per))

            carry = lax.fori_loop(0, ref.shape[0] // step, body, carry)
    logs = [jnp.zeros((NOTE_ROWS, rows), jnp.float32)] * len(outs)
    place = lax.broadcasted_iota(jnp.int32, (NOTE_ROWS, rows), 0)
    for i, (top, total, summed) in enumerate(carry):
        found = total > 0.0
        summed = summed * jnp.where(found, 1.0 / jnp.where(found, total, 1.0), 0.0)
        log = jnp.where(found, top + jnp.log(jnp.where(found, total, 1.0)), -big)
        first = log.astype(jnp.bfloat16).astype(jnp.float32)
        second = (log - first).astype(jnp.bfloat16).astype(jnp.float32)
        for k, out in enumerate(outs):
            at = slice(k * rows, (k + 1) * rows)
            out[i * HD : (i + 1) * HD, :] = summed[:, at].astype(jnp.bfloat16)
            for j, term in enumerate((first, second, log - first - second)):
                logs[k] = jnp.where(place == 3 * i + j, term[:, at], logs[k])
    for k, out in enumerate(outs):
        out[per * HD : per * HD + NOTE_ROWS, :] = logs[k].astype(jnp.bfloat16)


def project_kernel(per, sum_ref, log_ref, w_out_ref, *refs):
    backs, (keep_ref, send_ref, attended, branch) = refs[:2], refs[2:]
    for bits, back in zip(BACK, backs):
        logs = back[per * HD : per * HD + NOTE_ROWS, :].astype(jnp.float32)
        for i in range(per):
            at = head_at(bits, i, per)
            prefix_log = logs[3 * i : 3 * i + 1, :] + logs[3 * i + 1 : 3 * i + 2, :] + logs[3 * i + 2 : 3 * i + 3, :]
            suffix_log = log_ref[pl.ds(lax.div(at, HD), 1), :]
            top = jnp.maximum(prefix_log, suffix_log)
            prefix_part = jnp.exp(prefix_log - top)
            suffix_part = jnp.exp(suffix_log - top)
            whole = prefix_part + suffix_part
            joined = (
                back[i * HD : (i + 1) * HD, :].astype(jnp.float32) * (prefix_part / whole)
                + sum_ref[pl.ds(at, HD), :] * (suffix_part / whole)
            )
            attended[pl.ds(at, HD), :] = joined.astype(jnp.bfloat16)
    branch[...] = dot(attended[...], w_out_ref[...], TN)
    half = keep_ref.shape[0]
    side = lax.rem(lax.axis_index("mp"), 2)
    keep_ref[...] = branch[pl.ds(pl.multiple_of(side * half, half), half), :]
    other = branch[pl.ds(pl.multiple_of((1 - side) * half, half), half), :]
    send_ref[...] = other.astype(jnp.bfloat16)


def own_half_kernel(half_ref, out_ref, sem):
    half = half_ref.shape[0]
    side = lax.rem(lax.axis_index("mp"), 2)
    rows = pl.ds(pl.multiple_of(side * half, half), half)
    copy = pltpu.make_async_copy(half_ref, out_ref.at[rows, :], sem.at[0])
    copy.start()
    copy.wait()


def other_half_kernel(half_ref, _, out_ref, sem):
    half = half_ref.shape[0]
    side = lax.rem(lax.axis_index("mp"), 2)
    rows = pl.ds(pl.multiple_of((1 - side) * half, half), half)
    copy = pltpu.make_async_copy(half_ref, out_ref.at[rows, :], sem.at[0])
    copy.start()
    copy.wait()


def call(kernel, outs, specs, scratch=(), out_specs=None, aliases=None, cost=0.001):
    def run(*args):
        pinned = [
            pltpu.with_memory_space_constraint(x, pltpu.HBM) if spec is HBM else x
            for x, spec in zip(args, specs)
        ]
        return inner(*pinned)

    inner = pl.pallas_call(
        kernel,
        out_shape=tuple(jax.ShapeDtypeStruct(s, t) for s, t in outs),
        in_specs=specs,
        out_specs=out_specs or (VMEM,) * len(outs),
        scratch_shapes=scratch,
        input_output_aliases=aliases or {},
        compiler_params=pltpu.CompilerParams(vmem_limit_bytes=40 * 1024 * 1024),
        cost_estimate=pl.CostEstimate(flops=int(cost * 10**9), bytes_accessed=1, transcendentals=0),
    )
    return run


def local(
    hidden_in,
    norm_gain,
    norm_bias,
    w_query,
    w_key,
    w_value,
    w_out,
    prefix_keys,
    prefix_values,
    segment,
    request_group,
    block_slot,
    block_live,
):
    bf16, f32, i32 = jnp.bfloat16, jnp.float32, jnp.int32
    rows, width = hidden_in.shape
    local_width = w_query.shape[1]
    heads = local_width // HD
    n_blk = lax.axis_size("blk")
    n_mp = lax.axis_size("mp")
    per = heads // 2
    step = 2 * HD * per + NOTE_ROWS
    side = lax.rem(lax.axis_index("mp"), 2)

    def exchange(x, bits, far=0, back=False):
        pairs = []
        for i in range(n_blk):
            square, pair, lane = i // 4, i // 2 % 2, i % 2
            for m in range(n_mp):
                other, core = m // 2, m % 2
                blk = (square ^ far) * 4 + (pair ^ bits) * 2 + core
                link = (i * n_mp + m, blk * n_mp + other * 2 + 1 - lane)
                pairs.append(link[::-1] if back else link)
        return lax.ppermute(x, ("blk", "mp"), pairs)

    def across(x, bit):
        return lax.ppermute(x, "blk", [(i, i ^ bit) for i in range(n_blk)])

    def across_mp(x, bit):
        return lax.ppermute(x, "mp", [(i, i ^ bit) for i in range(n_mp)])

    group = jnp.where(block_live == 1, block_slot * GROUPS // n_blk, -1).astype(bf16)
    tag = jnp.broadcast_to(group, (NOTE_ROWS, HD))
    early = call(
        functools.partial(pack_kernel, per),
        [((step, HD), bf16)] * (3 if n_blk == 8 else 1),
        (HBM, HBM, VMEM),
        [pltpu.SemaphoreType.DMA(((6 if n_blk == 8 else 2) * per,))],
    )(prefix_keys, prefix_values, tag)
    near = exchange(early[0], 1)
    fars = [exchange(early[1 + k], k, far=1) for k in (0, 1)] if n_blk == 8 else []
    normed, query, *packs = call(
        functools.partial(query_kernel, per),
        [((rows, width), bf16), ((rows, local_width), bf16)]
        + [((per * rows + n, HD), bf16) for n in (step, NOTE_ROWS)],
        (HBM, HBM, VMEM) + (HBM,) * 6,
        [
            pltpu.VMEM((rows, width), bf16),
            pltpu.VMEM(w_query.shape, bf16),
            pltpu.VMEM((1, width), f32),
            pltpu.VMEM((1, width), f32),
            pltpu.VMEM(segment.shape, i32),
            pltpu.SMEM(request_group.shape, i32),
            pltpu.SemaphoreType.DMA((4 + ROW_CUTS + W_CUTS + 2 * per,)),
        ],
        cost=Q,
    )(
        prefix_keys,
        prefix_values,
        tag,
        hidden_in,
        w_query,
        norm_gain.reshape(1, width),
        norm_bias.reshape(1, width),
        segment,
        request_group,
    )
    asks = [exchange(packs[k], k) for k in ORDER]
    suffix_sum, suffix_log = call(
        functools.partial(suffix_kernel, heads),
        [((local_width, rows), f32), ((max(heads, 8), rows), f32)],
        (VMEM,) * 2 + (HBM,) * 3,
        [
            pltpu.VMEM(segment.shape, i32),
            pltpu.VMEM(w_key.shape, bf16),
            pltpu.VMEM(w_value.shape, bf16),
            pltpu.SemaphoreType.DMA((1 + 2 * W_CUTS,)),
        ],
        cost=SFX,
    )(normed, query, segment, w_key, w_value)
    last = asks[1][per * rows :]
    if fars:
        join = call(join_kernel, [((2 * step, HD), bf16)], (VMEM,) * 3, cost=JOIN1)
        first = join(suffix_log, fars[0], near)[0]
        first_other = across_mp(first, 1)
        wait = call(join_kernel, [((step, HD), bf16)], (VMEM,) * 2, cost=JOIN)
        second = wait(first, fars[1])[0]
        blocks = [first, first_other, second]
        others = [across_mp(x, 1) for x in (second, last)]
    else:
        blocks = [near, across_mp(near, 1)]
        others, bit = [across_mp(last, 1)], 4
        while bit < n_blk:
            others = others + [across(jnp.concatenate(blocks + [last] + others, axis=0), bit)]
            bit *= 2
    state, summed = call(
        functools.partial(first_kernel, rows, per),
        [((8, heads * rows), f32), ((HD, heads * rows), f32)],
        (VMEM,) * (2 + len(blocks)),
        cost=30,
    )(*asks, *blocks)
    backs = call(
        functools.partial(second_kernel, rows, per),
        [((per * HD + NOTE_ROWS, rows), bf16)] * 2,
        (VMEM,) * (4 + len(others)),
    )(*asks, state, summed, *others)
    backs = dict(zip(ORDER, backs))
    backs = [exchange(backs[k], k, back=True) for k in BACK]

    keep, send = call(
        functools.partial(project_kernel, per),
        [((rows // 2, width), f32), ((rows // 2, width), bf16)],
        (VMEM,) * 5,
        [pltpu.VMEM((local_width, rows), bf16), pltpu.VMEM((rows, width), f32)],
    )(suffix_sum, suffix_log, w_out, *backs)

    mine = (keep + across_mp(send, 1).astype(f32)).astype(bf16)
    bit = 2
    while bit < n_mp:
        mine = (mine.astype(f32) + across_mp(mine, bit).astype(f32)).astype(bf16 if 2 * bit < n_mp else f32)
        bit *= 2
    inputs = lax.dynamic_slice_in_dim(hidden_in, side * (rows // 2), rows // 2, 0)
    done = (inputs.astype(f32) + mine.astype(f32)).astype(bf16)
    other = across_mp(done, 1)
    whole = call(
        own_half_kernel,
        [((rows, width), bf16)],
        (VMEM,),
        [pltpu.SemaphoreType.DMA((1,))],
        (HBM,),
    )(done)[0]
    return call(
        other_half_kernel,
        [((rows, width), bf16)],
        (VMEM, HBM),
        [pltpu.SemaphoreType.DMA((1,))],
        (HBM,),
        {1: 0},
    )(other, whole)[0]


def solution(mesh):
    return jax.shard_map(
        local,
        mesh=mesh,
        in_specs=(
            P("blk", None),
            P(),
            P(),
            P(None, "mp"),
            P(None, "mp"),
            P(None, "mp"),
            P("mp", None),
            P("blk", None, "mp"),
            P("blk", None, "mp"),
            P("blk", None),
            P("blk", None),
            P("blk"),
            P("blk"),
        ),
        out_specs=P("blk", None),
        check_vma=False,
    )
```

```python
import functools

import jax
import jax.numpy as jnp
from jax import lax
from jax.experimental import pallas as pl
from jax.experimental.pallas import tpu as pltpu
from jax.sharding import PartitionSpec as P

HD = 128
GROUPS = 4
NOTE_ROWS = 16
ASK_ROWS = NOTE_ROWS + 128
W_CUTS = 4
ROW_CUTS = 2

ORDER = (1, 0)
BACK = (0, 1)

big = 1e30
Q = 0.001
SFX = 0.001
JOIN = 30
JOIN1 = 0.001

VMEM = pl.BlockSpec(memory_space=pltpu.VMEM)
HBM = pl.BlockSpec(memory_space=pltpu.HBM)
NT = (((1,), (1,)), ((), ()))
TN = (((0,), (0,)), ((), ()))


def dot(a, b, dims=(((1,), (0,)), ((), ()))):
    return lax.dot_general(a, b, dims, preferred_element_type=jnp.float32)


def head_at(bits, i, per):
    pair = lax.rem(lax.div(lax.axis_index("blk"), 2), 2)
    return pl.multiple_of(((pair ^ bits) * per + i) * HD, HD)


def start_all(pairs, sems):
    copies = [pltpu.make_async_copy(a, b, sems.at[i]) for i, (a, b) in enumerate(pairs)]
    for copy in copies:
        copy.start()
    return copies


def block_copies(per, bits, keys_ref, values_ref, out, at):
    pairs = []
    for i in range(per):
        cols = pl.ds(head_at(bits, i, per), HD)
        pairs.append((keys_ref.at[0, :, cols], out.at[at : at + HD, :]))
        pairs.append((values_ref.at[0, :, cols], out.at[at + HD : at + 2 * HD, :]))
        at += 2 * HD
    return pairs


def pack_kernel(per, keys_ref, values_ref, tag_ref, *refs):
    outs, sems = refs[:-1], refs[-1]
    pairs = []
    for bits, out in zip((1, 0, 1), outs):
        pairs += block_copies(per, bits, keys_ref, values_ref, out, 0)
    copies = start_all(pairs, sems)
    for out in outs:
        out[2 * HD * per : 2 * HD * per + NOTE_ROWS, :] = tag_ref[...]
    for copy in copies:
        copy.wait()


def join_kernel(_, *refs):
    out = refs[-1]
    for i, ref in enumerate(refs[:-1]):
        out[i * ref.shape[0] : (i + 1) * ref.shape[0], :] = ref[...]


def gate_kernel(*refs):
    refs[-1][...] = jnp.zeros_like(refs[-1])


def last_join_kernel(_, far_ref, ask_ref, out):
    step = far_ref.shape[0]
    out[0:step, :] = far_ref[...]
    out[step : 2 * step, :] = ask_ref[ask_ref.shape[0] - step :, :]


def query_kernel(per, *refs):
    keys_ref, values_ref, tag_ref, hidden_in, w_query, *sources = refs[:9]
    normed_ref, query_ref = refs[9:11]
    outs, held, sems = refs[11:13], refs[13:-1], refs[-1]
    hidden_ref, w_query_ref, gain_ref, bias_ref, segment_ref, request_group_ref = held
    rows, width = hidden_ref.shape
    row_cuts = [pl.ds(i * (rows // ROW_CUTS), rows // ROW_CUTS) for i in range(ROW_CUTS)]
    w_cuts = [pl.ds(i * (width // W_CUTS), width // W_CUTS) for i in range(W_CUTS)]
    pairs = [(hidden_in.at[cut, :], hidden_ref.at[cut, :]) for cut in row_cuts]
    pairs += list(zip(sources, held[2:]))
    pairs += [(w_query.at[cut, :], w_query_ref.at[cut, :]) for cut in w_cuts]
    pairs += block_copies(per, 0, keys_ref, values_ref, outs[0], per * rows)
    copies = start_all(pairs, sems)
    small = copies[ROW_CUTS : ROW_CUTS + 4]
    weights = copies[ROW_CUTS + 4 : ROW_CUTS + 4 + W_CUTS]
    for cut, copy in zip(row_cuts, copies):
        copy.wait()
        if cut is row_cuts[0]:
            small[0].wait()
            small[1].wait()
        inputs = hidden_ref[cut, :].astype(jnp.float32)
        mean = jnp.mean(inputs, axis=-1, keepdims=True)
        centred = inputs - mean
        var = jnp.mean(centred * centred, axis=-1, keepdims=True)
        normed = centred * lax.rsqrt(var + 1e-05) * gain_ref[...] + bias_ref[...]
        normed_ref[cut, :] = normed.astype(jnp.bfloat16)
    small[2].wait()
    small[3].wait()
    segment = segment_ref[...]
    group = jnp.zeros_like(segment)
    for r in range(request_group_ref.shape[1]):
        group = jnp.where(segment == r, request_group_ref[0, r], group)
    tag = tag_ref[...].astype(jnp.float32)
    place = lax.broadcasted_iota(jnp.int32, tag.shape, 0)
    notes = jnp.where(place == 0, tag, group.astype(jnp.float32)).astype(jnp.bfloat16)
    query = jnp.zeros(query_ref.shape, jnp.float32)
    for cut, copy in zip(w_cuts, weights):
        copy.wait()
        query = query + dot(normed_ref[:, cut], w_query_ref[cut, :])
    query_ref[...] = (query * (HD**-0.5)).astype(jnp.bfloat16)
    for bits, out in enumerate(outs):
        for i in range(per):
            out[i * rows : (i + 1) * rows, :] = query_ref[:, pl.ds(head_at(bits, i, per), HD)]
        out[out.shape[0] - NOTE_ROWS : out.shape[0], :] = notes
    for copy in copies[ROW_CUTS + 4 + W_CUTS :]:
        copy.wait()


def suffix_kernel(heads, normed_ref, query_ref, *refs):
    sources, (sum_ref, log_ref), held, sems = refs[:3], refs[3:5], refs[5:8], refs[8]
    segment_ref, w_key_ref, w_value_ref = held
    rows, width = normed_ref.shape
    cut = width // W_CUTS
    pairs = [(sources[0], held[0])]
    for source, target in zip(sources[1:], held[1:]):
        parts = [pl.ds(i * cut, cut) for i in range(W_CUTS)]
        pairs += [(source.at[part, :], target.at[part, :]) for part in parts]
    copies = start_all(pairs, sems)

    def project(target, waits):
        out = jnp.zeros((rows, target.shape[1]), jnp.float32)
        for i, copy in enumerate(waits):
            copy.wait()
            at = slice(i * cut, (i + 1) * cut)
            out = out + dot(normed_ref[:, at], target[at, :])
        return out.astype(jnp.bfloat16)

    key = project(w_key_ref, copies[1 : 1 + W_CUTS])
    value = project(w_value_ref, copies[1 + W_CUTS :])
    copies[0].wait()
    by_token = jnp.broadcast_to(segment_ref[...], (rows, rows))
    key_place = lax.broadcasted_iota(jnp.int32, (rows, rows), 0)
    token_place = lax.broadcasted_iota(jnp.int32, (rows, rows), 1)
    by_key = jnp.sum(
        jnp.where(key_place == token_place, by_token, 0).astype(jnp.float32), axis=1, keepdims=True
    )
    mask = (by_key == by_token.astype(jnp.float32)) & (key_place <= token_place)
    for h in range(heads):
        cols = slice(h * HD, (h + 1) * HD)
        scores = jnp.where(mask, dot(key[:, cols], query_ref[:, cols], NT), -big)
        top = jnp.max(scores, axis=0, keepdims=True)
        weights = jnp.exp(scores - top)
        total = jnp.sum(weights, axis=0, keepdims=True)
        summed = dot(value[:, cols], weights.astype(jnp.bfloat16), TN)
        sum_ref[cols, :] = summed / total
        log_ref[h : h + 1, :] = top + jnp.log(total)


def absorb(carry, found):
    top, total, summed = carry
    new_top = top
    for scores, mask, _ in found:
        best = jnp.max(scores, axis=0, keepdims=True)
        new_top = jnp.maximum(new_top, jnp.where(mask, best, -big))
    factor = jnp.exp(top - new_top)
    total, summed = total * factor, summed * factor
    for scores, mask, values in found:
        weights = jnp.exp(scores - jnp.where(mask, new_top, big))
        total = total + jnp.sum(weights, axis=0, keepdims=True)
        summed = summed + dot(values, weights.astype(jnp.bfloat16), TN)
    return new_top, total, summed


def questions(asks, rows, per):
    queries = [
        jnp.concatenate([ref[i * rows : (i + 1) * rows, :] for ref in asks], axis=0) for i in range(per)
    ]
    notes = [ref[ref.shape[0] - NOTE_ROWS : ref.shape[0], :].astype(jnp.float32)[1:2, :] for ref in asks]
    return queries, jnp.concatenate(notes, axis=1)


def block_scores(ref, at, queries, group):
    per = len(queries)
    tag = ref[pl.ds(at + 2 * HD * per, NOTE_ROWS), :].astype(jnp.float32)[0:1, 0:1]
    found = []
    for i, query in enumerate(queries):
        keys, values = (ref[pl.ds(at + j * HD, HD), :] for j in (2 * i, 2 * i + 1))
        found.append((dot(keys, query, NT), group == tag, values))
    return found


def first_kernel(rows, per, *refs):
    asks, early, (state_ref, sum_ref) = refs[1::-1], refs[2:-2], refs[-2:]
    queries, group = questions(asks, rows, per)
    tokens = group.shape[1]
    step = 2 * HD * per + NOTE_ROWS
    found = [] if early[2:] else [block_scores(asks[1], per * rows, queries, group)]
    for ref in early:
        found += [block_scores(ref, at, queries, group) for at in range(0, ref.shape[0], step)]
    for i in range(per):
        carry = (
            jnp.full((1, tokens), -big, jnp.float32),
            jnp.zeros((1, tokens), jnp.float32),
            jnp.zeros((HD, tokens), jnp.float32),
        )
        top, total, summed = absorb(carry, [block[i] for block in found])
        cols = slice(i * tokens, (i + 1) * tokens)
        state_ref[0:1, cols] = top
        state_ref[1:2, cols] = total
        sum_ref[:, cols] = summed


def second_kernel(rows, per, *refs):
    asks, (state_ref, sum_ref), blocks, outs = refs[1::-1], refs[2:4], refs[4:-2], refs[-2:]
    queries, group = questions(asks, rows, per)
    tokens = group.shape[1]
    step = 2 * HD * per + NOTE_ROWS
    cols = [slice(i * tokens, (i + 1) * tokens) for i in range(per)]
    carry = [(state_ref[0:1, at], state_ref[1:2, at], sum_ref[:, at]) for at in cols]
    found = [
        block_scores(ref, at, queries, group)
        for ref in blocks
        if ref.shape[0] <= 3 * step
        for at in range(0, ref.shape[0], step)
    ]
    carry = tuple(absorb(carry[i], [block[i] for block in found]) for i in range(per))
    for ref in blocks:
        if ref.shape[0] > 3 * step:

            def body(b, state, ref=ref):
                block = block_scores(ref, pl.multiple_of(b * step, NOTE_ROWS), queries, group)
                return tuple(absorb(state[i], [block[i]]) for i in range(per))

            carry = lax.fori_loop(0, ref.shape[0] // step, body, carry)
    logs = [jnp.zeros((NOTE_ROWS, rows), jnp.float32)] * len(outs)
    place = lax.broadcasted_iota(jnp.int32, (NOTE_ROWS, rows), 0)
    for i, (top, total, summed) in enumerate(carry):
        found = total > 0.0
        summed = summed * jnp.where(found, 1.0 / jnp.where(found, total, 1.0), 0.0)
        log = jnp.where(found, top + jnp.log(jnp.where(found, total, 1.0)), -big)
        first = log.astype(jnp.bfloat16).astype(jnp.float32)
        second = (log - first).astype(jnp.bfloat16).astype(jnp.float32)
        for k, out in enumerate(outs):
            at = slice(k * rows, (k + 1) * rows)
            out[i * HD : (i + 1) * HD, :] = summed[:, at].astype(jnp.bfloat16)
            for j, term in enumerate((first, second, log - first - second)):
                logs[k] = jnp.where(place == 3 * i + j, term[:, at], logs[k])
    for k, out in enumerate(outs):
        out[per * HD : per * HD + NOTE_ROWS, :] = logs[k].astype(jnp.bfloat16)


def project_kernel(per, sum_ref, log_ref, w_out_ref, *refs):
    backs, (keep_ref, send_ref, attended, branch) = refs[:2], refs[2:]
    for bits, back in zip(BACK, backs):
        logs = back[per * HD : per * HD + NOTE_ROWS, :].astype(jnp.float32)
        for i in range(per):
            at = head_at(bits, i, per)
            prefix_log = logs[3 * i : 3 * i + 1, :] + logs[3 * i + 1 : 3 * i + 2, :] + logs[3 * i + 2 : 3 * i + 3, :]
            suffix_log = log_ref[pl.ds(lax.div(at, HD), 1), :]
            top = jnp.maximum(prefix_log, suffix_log)
            prefix_part = jnp.exp(prefix_log - top)
            suffix_part = jnp.exp(suffix_log - top)
            whole = prefix_part + suffix_part
            joined = (
                back[i * HD : (i + 1) * HD, :].astype(jnp.float32) * (prefix_part / whole)
                + sum_ref[pl.ds(at, HD), :] * (suffix_part / whole)
            )
            attended[pl.ds(at, HD), :] = joined.astype(jnp.bfloat16)
    branch[...] = dot(attended[...], w_out_ref[...], TN)
    half = keep_ref.shape[0]
    side = lax.rem(lax.axis_index("mp"), 2)
    keep_ref[...] = branch[pl.ds(pl.multiple_of(side * half, half), half), :]
    other = branch[pl.ds(pl.multiple_of((1 - side) * half, half), half), :]
    send_ref[...] = other.astype(jnp.bfloat16)


def own_half_kernel(half_ref, out_ref, sem):
    half = half_ref.shape[0]
    side = lax.rem(lax.axis_index("mp"), 2)
    rows = pl.ds(pl.multiple_of(side * half, half), half)
    copy = pltpu.make_async_copy(half_ref, out_ref.at[rows, :], sem.at[0])
    copy.start()
    copy.wait()


def other_half_kernel(half_ref, _, out_ref, sem):
    half = half_ref.shape[0]
    side = lax.rem(lax.axis_index("mp"), 2)
    rows = pl.ds(pl.multiple_of((1 - side) * half, half), half)
    copy = pltpu.make_async_copy(half_ref, out_ref.at[rows, :], sem.at[0])
    copy.start()
    copy.wait()


def call(kernel, outs, specs, scratch=(), out_specs=None, aliases=None, cost=0.001):
    def run(*args):
        pinned = [
            pltpu.with_memory_space_constraint(x, pltpu.HBM) if spec is HBM else x
            for x, spec in zip(args, specs)
        ]
        return inner(*pinned)

    inner = pl.pallas_call(
        kernel,
        out_shape=tuple(jax.ShapeDtypeStruct(s, t) for s, t in outs),
        in_specs=specs,
        out_specs=out_specs or (VMEM,) * len(outs),
        scratch_shapes=scratch,
        input_output_aliases=aliases or {},
        compiler_params=pltpu.CompilerParams(vmem_limit_bytes=40 * 1024 * 1024),
        cost_estimate=pl.CostEstimate(flops=int(cost * 10**9), bytes_accessed=1, transcendentals=0),
    )
    return run


def local(
    hidden_in,
    norm_gain,
    norm_bias,
    w_query,
    w_key,
    w_value,
    w_out,
    prefix_keys,
    prefix_values,
    segment,
    request_group,
    block_slot,
    block_live,
):
    bf16, f32, i32 = jnp.bfloat16, jnp.float32, jnp.int32
    rows, width = hidden_in.shape
    local_width = w_query.shape[1]
    heads = local_width // HD
    n_blk = lax.axis_size("blk")
    n_mp = lax.axis_size("mp")
    per = heads // 2
    step = 2 * HD * per + NOTE_ROWS
    side = lax.rem(lax.axis_index("mp"), 2)

    def exchange(x, bits, far=0, back=False):
        pairs = []
        for i in range(n_blk):
            square, pair, lane = i // 4, i // 2 % 2, i % 2
            for m in range(n_mp):
                other, core = m // 2, m % 2
                blk = (square ^ far) * 4 + (pair ^ bits) * 2 + 1 - core
                link = (i * n_mp + m, blk * n_mp + other * 2 + lane)
                pairs.append(link[::-1] if back else link)
        return lax.ppermute(x, ("blk", "mp"), pairs)

    def across(x, bit):
        return lax.ppermute(x, "blk", [(i, i ^ bit) for i in range(n_blk)])

    def across_mp(x, bit):
        return lax.ppermute(x, "mp", [(i, i ^ bit) for i in range(n_mp)])

    group = jnp.where(block_live == 1, block_slot * GROUPS // n_blk, -1).astype(bf16)
    tag = jnp.broadcast_to(group, (NOTE_ROWS, HD))
    early = call(
        functools.partial(pack_kernel, per),
        [((step, HD), bf16)] * (3 if n_blk == 8 else 1),
        (HBM, HBM, VMEM),
        [pltpu.SemaphoreType.DMA(((6 if n_blk == 8 else 2) * per,))],
    )(prefix_keys, prefix_values, tag)
    near = exchange(early[0], 1)
    fars = [exchange(early[1 + k], k, far=1) for k in (0, 1)] if n_blk == 8 else []
    normed, query, *packs = call(
        functools.partial(query_kernel, per),
        [((rows, width), bf16), ((rows, local_width), bf16)]
        + [((per * rows + n, HD), bf16) for n in (step, NOTE_ROWS)],
        (HBM, HBM, VMEM) + (HBM,) * 6,
        [
            pltpu.VMEM((rows, width), bf16),
            pltpu.VMEM(w_query.shape, bf16),
            pltpu.VMEM((1, width), f32),
            pltpu.VMEM((1, width), f32),
            pltpu.VMEM(segment.shape, i32),
            pltpu.SMEM(request_group.shape, i32),
            pltpu.SemaphoreType.DMA((4 + ROW_CUTS + W_CUTS + 2 * per,)),
        ],
        cost=Q,
    )(
        prefix_keys,
        prefix_values,
        tag,
        hidden_in,
        w_query,
        norm_gain.reshape(1, width),
        norm_bias.reshape(1, width),
        segment,
        request_group,
    )
    asks = {k: exchange(packs[k], k) for k in ORDER[::-1]}
    asks = [asks[k] for k in ORDER]
    suffix_sum, suffix_log = call(
        functools.partial(suffix_kernel, heads),
        [((local_width, rows), f32), ((max(heads, 8), rows), f32)],
        (VMEM,) * 2 + (HBM,) * 3,
        [
            pltpu.VMEM(segment.shape, i32),
            pltpu.VMEM(w_key.shape, bf16),
            pltpu.VMEM(w_value.shape, bf16),
            pltpu.SemaphoreType.DMA((1 + 2 * W_CUTS,)),
        ],
        cost=SFX,
    )(normed, query, segment, w_key, w_value)
    last = asks[1][per * rows :]
    if fars:
        join = call(join_kernel, [((2 * step, HD), bf16)], (VMEM,) * 3, cost=JOIN1)
        first = join(suffix_log, fars[0], near)[0]
        first_other = across_mp(first, 1)
        wait = call(gate_kernel, [((8, HD), f32)], (VMEM,) * 2, cost=JOIN)
        gate = wait(first, fars[1])[0]
        second = call(last_join_kernel, [((2 * step, HD), bf16)], (VMEM,) * 3)(gate, fars[1], asks[1])[0]
        blocks = [first, first_other, second]
        others = [across_mp(second, 1)]
    else:
        blocks = [near, across_mp(near, 1)]
        others, bit = [across_mp(last, 1)], 4
        while bit < n_blk:
            others = others + [across(jnp.concatenate(blocks + [last] + others, axis=0), bit)]
            bit *= 2
    state, summed = call(
        functools.partial(first_kernel, rows, per),
        [((8, heads * rows), f32), ((HD, heads * rows), f32)],
        (VMEM,) * (2 + len(blocks)),
        cost=30,
    )(*asks[::-1], *blocks)
    backs = call(
        functools.partial(second_kernel, rows, per),
        [((per * HD + NOTE_ROWS, rows), bf16)] * 2,
        (VMEM,) * (4 + len(others)),
    )(*asks[::-1], state, summed, *others)
    backs = dict(zip(ORDER, backs))
    backs = [exchange(backs[k], k, back=True) for k in BACK]

    keep, send = call(
        functools.partial(project_kernel, per),
        [((rows // 2, width), f32), ((rows // 2, width), bf16)],
        (VMEM,) * 5,
        [pltpu.VMEM((local_width, rows), bf16), pltpu.VMEM((rows, width), f32)],
    )(suffix_sum, suffix_log, w_out, *backs)

    mine = (keep + across_mp(send, 1).astype(f32)).astype(bf16)
    bit = 2
    while bit < n_mp:
        mine = (mine.astype(f32) + across_mp(mine, bit).astype(f32)).astype(bf16 if 2 * bit < n_mp else f32)
        bit *= 2
    inputs = lax.dynamic_slice_in_dim(hidden_in, side * (rows // 2), rows // 2, 0)
    done = (inputs.astype(f32) + mine.astype(f32)).astype(bf16)
    other = across_mp(done, 1)
    whole = call(
        own_half_kernel,
        [((rows, width), bf16)],
        (VMEM,),
        [pltpu.SemaphoreType.DMA((1,))],
        (HBM,),
    )(done)[0]
    return call(
        other_half_kernel,
        [((rows, width), bf16)],
        (VMEM, HBM),
        [pltpu.SemaphoreType.DMA((1,))],
        (HBM,),
        {1: 0},
    )(other, whole)[0]


def solution(mesh):
    return jax.shard_map(
        local,
        mesh=mesh,
        in_specs=(
            P("blk", None),
            P(),
            P(),
            P(None, "mp"),
            P(None, "mp"),
            P(None, "mp"),
            P("mp", None),
            P("blk", None, "mp"),
            P("blk", None, "mp"),
            P("blk", None),
            P("blk", None),
            P("blk"),
            P("blk"),
        ),
        out_specs=P("blk", None),
        check_vma=False,
    )
```

```python
import functools

import jax
import jax.numpy as jnp
from jax import lax
from jax.experimental import pallas as pl
from jax.experimental.pallas import tpu as pltpu
from jax.sharding import PartitionSpec as P

HD = 128
GROUPS = 4
NOTE_ROWS = 16
ASK_ROWS = NOTE_ROWS + 128
W_CUTS = 2
ROW_CUTS = 1

ORDER = (1, 0)
BACK = (0, 1)

big = 1e30
Q = 0.001
SFX = 0.001
JOIN = 30
JOIN1 = 0.001

VMEM = pl.BlockSpec(memory_space=pltpu.VMEM)
HBM = pl.BlockSpec(memory_space=pltpu.HBM)
NT = (((1,), (1,)), ((), ()))
TN = (((0,), (0,)), ((), ()))


def dot(a, b, dims=(((1,), (0,)), ((), ()))):
    return lax.dot_general(a, b, dims, preferred_element_type=jnp.float32)


def head_at(bits, i, per):
    pair = lax.rem(lax.div(lax.axis_index("blk"), 2), 2)
    return pl.multiple_of(((pair ^ bits) * per + i) * HD, HD)


def start_all(pairs, sems):
    copies = [pltpu.make_async_copy(a, b, sems.at[i]) for i, (a, b) in enumerate(pairs)]
    for copy in copies:
        copy.start()
    return copies


def block_copies(per, bits, keys_ref, values_ref, out, at):
    pairs = []
    for i in range(per):
        cols = pl.ds(head_at(bits, i, per), HD)
        pairs.append((keys_ref.at[0, :, cols], out.at[at : at + HD, :]))
        pairs.append((values_ref.at[0, :, cols], out.at[at + HD : at + 2 * HD, :]))
        at += 2 * HD
    return pairs


def pack_kernel(per, keys_ref, values_ref, tag_ref, *refs):
    outs, sems = refs[:-1], refs[-1]
    pairs = []
    for bits, out in zip((1, 0, 1), outs):
        pairs += block_copies(per, bits, keys_ref, values_ref, out, 0)
    copies = start_all(pairs, sems)
    for out in outs:
        out[2 * HD * per : 2 * HD * per + NOTE_ROWS, :] = tag_ref[...]
    for copy in copies:
        copy.wait()


def join_kernel(_, *refs):
    out = refs[-1]
    for i, ref in enumerate(refs[:-1]):
        out[i * ref.shape[0] : (i + 1) * ref.shape[0], :] = ref[...]


def gate_kernel(*refs):
    refs[-1][...] = jnp.zeros_like(refs[-1])


def last_join_kernel(_, far_ref, ask_ref, out):
    step = far_ref.shape[0]
    out[0:step, :] = far_ref[...]
    out[step : 2 * step, :] = ask_ref[ask_ref.shape[0] - step :, :]


def query_kernel(per, *refs):
    keys_ref, values_ref, tag_ref, hidden_in, w_query, *sources = refs[:9]
    normed_ref, query_ref = refs[9:11]
    outs, held, sems = refs[11:13], refs[13:-1], refs[-1]
    hidden_ref, w_query_ref, gain_ref, bias_ref, segment_ref, request_group_ref = held
    rows, width = hidden_ref.shape
    row_cuts = [pl.ds(i * (rows // ROW_CUTS), rows // ROW_CUTS) for i in range(ROW_CUTS)]
    w_cuts = [pl.ds(i * (width // W_CUTS), width // W_CUTS) for i in range(W_CUTS)]
    pairs = [(hidden_in.at[cut, :], hidden_ref.at[cut, :]) for cut in row_cuts]
    pairs += list(zip(sources, held[2:]))
    pairs += [(w_query.at[cut, :], w_query_ref.at[cut, :]) for cut in w_cuts]
    pairs += block_copies(per, 0, keys_ref, values_ref, outs[0], per * rows)
    copies = start_all(pairs, sems)
    small = copies[ROW_CUTS : ROW_CUTS + 4]
    weights = copies[ROW_CUTS + 4 : ROW_CUTS + 4 + W_CUTS]
    for cut, copy in zip(row_cuts, copies):
        copy.wait()
        if cut is row_cuts[0]:
            small[0].wait()
            small[1].wait()
        inputs = hidden_ref[cut, :].astype(jnp.float32)
        mean = jnp.mean(inputs, axis=-1, keepdims=True)
        centred = inputs - mean
        var = jnp.mean(centred * centred, axis=-1, keepdims=True)
        normed = centred * lax.rsqrt(var + 1e-05) * gain_ref[...] + bias_ref[...]
        normed_ref[cut, :] = normed.astype(jnp.bfloat16)
    small[2].wait()
    small[3].wait()
    segment = segment_ref[...]
    group = jnp.zeros_like(segment)
    for r in range(request_group_ref.shape[1]):
        group = jnp.where(segment == r, request_group_ref[0, r], group)
    tag = tag_ref[...].astype(jnp.float32)
    place = lax.broadcasted_iota(jnp.int32, tag.shape, 0)
    notes = jnp.where(place == 0, tag, group.astype(jnp.float32)).astype(jnp.bfloat16)
    query = jnp.zeros(query_ref.shape, jnp.float32)
    for cut, copy in zip(w_cuts, weights):
        copy.wait()
        query = query + dot(normed_ref[:, cut], w_query_ref[cut, :])
    query_ref[...] = (query * (HD**-0.5)).astype(jnp.bfloat16)
    for bits, out in enumerate(outs):
        for i in range(per):
            out[i * rows : (i + 1) * rows, :] = query_ref[:, pl.ds(head_at(bits, i, per), HD)]
        out[out.shape[0] - NOTE_ROWS : out.shape[0], :] = notes
    for copy in copies[ROW_CUTS + 4 + W_CUTS :]:
        copy.wait()


def suffix_kernel(heads, normed_ref, query_ref, *refs):
    sources, (sum_ref, log_ref), held, sems = refs[:3], refs[3:5], refs[5:8], refs[8]
    segment_ref, w_key_ref, w_value_ref = held
    rows, width = normed_ref.shape
    cut = width // W_CUTS
    pairs = [(sources[0], held[0])]
    for source, target in zip(sources[1:], held[1:]):
        parts = [pl.ds(i * cut, cut) for i in range(W_CUTS)]
        pairs += [(source.at[part, :], target.at[part, :]) for part in parts]
    copies = start_all(pairs, sems)

    def project(target, waits):
        out = jnp.zeros((rows, target.shape[1]), jnp.float32)
        for i, copy in enumerate(waits):
            copy.wait()
            at = slice(i * cut, (i + 1) * cut)
            out = out + dot(normed_ref[:, at], target[at, :])
        return out.astype(jnp.bfloat16)

    key = project(w_key_ref, copies[1 : 1 + W_CUTS])
    value = project(w_value_ref, copies[1 + W_CUTS :])
    copies[0].wait()
    by_token = jnp.broadcast_to(segment_ref[...], (rows, rows))
    key_place = lax.broadcasted_iota(jnp.int32, (rows, rows), 0)
    token_place = lax.broadcasted_iota(jnp.int32, (rows, rows), 1)
    by_key = jnp.sum(
        jnp.where(key_place == token_place, by_token, 0).astype(jnp.float32), axis=1, keepdims=True
    )
    mask = (by_key == by_token.astype(jnp.float32)) & (key_place <= token_place)
    for h in range(heads):
        cols = slice(h * HD, (h + 1) * HD)
        scores = jnp.where(mask, dot(key[:, cols], query_ref[:, cols], NT), -big)
        top = jnp.max(scores, axis=0, keepdims=True)
        weights = jnp.exp(scores - top)
        total = jnp.sum(weights, axis=0, keepdims=True)
        summed = dot(value[:, cols], weights.astype(jnp.bfloat16), TN)
        sum_ref[cols, :] = summed / total
        log_ref[h : h + 1, :] = top + jnp.log(total)


def absorb(carry, found):
    top, total, summed = carry
    new_top = top
    for scores, mask, _ in found:
        best = jnp.max(scores, axis=0, keepdims=True)
        new_top = jnp.maximum(new_top, jnp.where(mask, best, -big))
    factor = jnp.exp(top - new_top)
    total, summed = total * factor, summed * factor
    for scores, mask, values in found:
        weights = jnp.exp(scores - jnp.where(mask, new_top, big))
        total = total + jnp.sum(weights, axis=0, keepdims=True)
        summed = summed + dot(values, weights.astype(jnp.bfloat16), TN)
    return new_top, total, summed


def questions(asks, rows, per):
    queries = [
        jnp.concatenate([ref[i * rows : (i + 1) * rows, :] for ref in asks], axis=0) for i in range(per)
    ]
    notes = [ref[ref.shape[0] - NOTE_ROWS : ref.shape[0], :].astype(jnp.float32)[1:2, :] for ref in asks]
    return queries, jnp.concatenate(notes, axis=1)


def block_scores(ref, at, queries, group):
    per = len(queries)
    tag = ref[pl.ds(at + 2 * HD * per, NOTE_ROWS), :].astype(jnp.float32)[0:1, 0:1]
    found = []
    for i, query in enumerate(queries):
        keys, values = (ref[pl.ds(at + j * HD, HD), :] for j in (2 * i, 2 * i + 1))
        found.append((dot(keys, query, NT), group == tag, values))
    return found


def first_kernel(rows, per, *refs):
    asks, early, (state_ref, sum_ref) = refs[1::-1], refs[2:-2], refs[-2:]
    queries, group = questions(asks, rows, per)
    tokens = group.shape[1]
    step = 2 * HD * per + NOTE_ROWS
    found = [] if early[2:] else [block_scores(asks[1], per * rows, queries, group)]
    for ref in early:
        found += [block_scores(ref, at, queries, group) for at in range(0, ref.shape[0], step)]
    for i in range(per):
        carry = (
            jnp.full((1, tokens), -big, jnp.float32),
            jnp.zeros((1, tokens), jnp.float32),
            jnp.zeros((HD, tokens), jnp.float32),
        )
        top, total, summed = absorb(carry, [block[i] for block in found])
        cols = slice(i * tokens, (i + 1) * tokens)
        state_ref[0:1, cols] = top
        state_ref[1:2, cols] = total
        sum_ref[:, cols] = summed


def second_kernel(rows, per, *refs):
    asks, (state_ref, sum_ref), blocks, outs = refs[1::-1], refs[2:4], refs[4:-2], refs[-2:]
    queries, group = questions(asks, rows, per)
    tokens = group.shape[1]
    step = 2 * HD * per + NOTE_ROWS
    cols = [slice(i * tokens, (i + 1) * tokens) for i in range(per)]
    carry = [(state_ref[0:1, at], state_ref[1:2, at], sum_ref[:, at]) for at in cols]
    found = [
        block_scores(ref, at, queries, group)
        for ref in blocks
        if ref.shape[0] <= 3 * step
        for at in range(0, ref.shape[0], step)
    ]
    carry = tuple(absorb(carry[i], [block[i] for block in found]) for i in range(per))
    for ref in blocks:
        if ref.shape[0] > 3 * step:

            def body(b, state, ref=ref):
                block = block_scores(ref, pl.multiple_of(b * step, NOTE_ROWS), queries, group)
                return tuple(absorb(state[i], [block[i]]) for i in range(per))

            carry = lax.fori_loop(0, ref.shape[0] // step, body, carry)
    logs = [jnp.zeros((NOTE_ROWS, rows), jnp.float32)] * len(outs)
    place = lax.broadcasted_iota(jnp.int32, (NOTE_ROWS, rows), 0)
    for i, (top, total, summed) in enumerate(carry):
        found = total > 0.0
        summed = summed * jnp.where(found, 1.0 / jnp.where(found, total, 1.0), 0.0)
        log = jnp.where(found, top + jnp.log(jnp.where(found, total, 1.0)), -big)
        first = log.astype(jnp.bfloat16).astype(jnp.float32)
        second = (log - first).astype(jnp.bfloat16).astype(jnp.float32)
        for k, out in enumerate(outs):
            at = slice(k * rows, (k + 1) * rows)
            out[i * HD : (i + 1) * HD, :] = summed[:, at].astype(jnp.bfloat16)
            for j, term in enumerate((first, second, log - first - second)):
                logs[k] = jnp.where(place == 3 * i + j, term[:, at], logs[k])
    for k, out in enumerate(outs):
        out[per * HD : per * HD + NOTE_ROWS, :] = logs[k].astype(jnp.bfloat16)


def project_kernel(per, sum_ref, log_ref, w_out_ref, *refs):
    backs, (keep_ref, send_ref, attended, branch) = refs[:2], refs[2:]
    for bits, back in zip(BACK, backs):
        logs = back[per * HD : per * HD + NOTE_ROWS, :].astype(jnp.float32)
        for i in range(per):
            at = head_at(bits, i, per)
            prefix_log = logs[3 * i : 3 * i + 1, :] + logs[3 * i + 1 : 3 * i + 2, :] + logs[3 * i + 2 : 3 * i + 3, :]
            suffix_log = log_ref[pl.ds(lax.div(at, HD), 1), :]
            top = jnp.maximum(prefix_log, suffix_log)
            prefix_part = jnp.exp(prefix_log - top)
            suffix_part = jnp.exp(suffix_log - top)
            whole = prefix_part + suffix_part
            joined = (
                back[i * HD : (i + 1) * HD, :].astype(jnp.float32) * (prefix_part / whole)
                + sum_ref[pl.ds(at, HD), :] * (suffix_part / whole)
            )
            attended[pl.ds(at, HD), :] = joined.astype(jnp.bfloat16)
    branch[...] = dot(attended[...], w_out_ref[...], TN)
    half = keep_ref.shape[0]
    side = lax.rem(lax.axis_index("mp"), 2)
    keep_ref[...] = branch[pl.ds(pl.multiple_of(side * half, half), half), :]
    other = branch[pl.ds(pl.multiple_of((1 - side) * half, half), half), :]
    send_ref[...] = other.astype(jnp.bfloat16)


def own_half_kernel(half_ref, out_ref, sem):
    half = half_ref.shape[0]
    side = lax.rem(lax.axis_index("mp"), 2)
    rows = pl.ds(pl.multiple_of(side * half, half), half)
    copy = pltpu.make_async_copy(half_ref, out_ref.at[rows, :], sem.at[0])
    copy.start()
    copy.wait()


def other_half_kernel(half_ref, _, out_ref, sem):
    half = half_ref.shape[0]
    side = lax.rem(lax.axis_index("mp"), 2)
    rows = pl.ds(pl.multiple_of((1 - side) * half, half), half)
    copy = pltpu.make_async_copy(half_ref, out_ref.at[rows, :], sem.at[0])
    copy.start()
    copy.wait()


def call(kernel, outs, specs, scratch=(), out_specs=None, aliases=None, cost=0.001):
    def run(*args):
        pinned = [
            pltpu.with_memory_space_constraint(x, pltpu.HBM) if spec is HBM else x
            for x, spec in zip(args, specs)
        ]
        return inner(*pinned)

    inner = pl.pallas_call(
        kernel,
        out_shape=tuple(jax.ShapeDtypeStruct(s, t) for s, t in outs),
        in_specs=specs,
        out_specs=out_specs or (VMEM,) * len(outs),
        scratch_shapes=scratch,
        input_output_aliases=aliases or {},
        compiler_params=pltpu.CompilerParams(vmem_limit_bytes=40 * 1024 * 1024),
        cost_estimate=pl.CostEstimate(flops=int(cost * 10**9), bytes_accessed=1, transcendentals=0),
    )
    return run


def local(
    hidden_in,
    norm_gain,
    norm_bias,
    w_query,
    w_key,
    w_value,
    w_out,
    prefix_keys,
    prefix_values,
    segment,
    request_group,
    block_slot,
    block_live,
):
    bf16, f32, i32 = jnp.bfloat16, jnp.float32, jnp.int32
    rows, width = hidden_in.shape
    local_width = w_query.shape[1]
    heads = local_width // HD
    n_blk = lax.axis_size("blk")
    n_mp = lax.axis_size("mp")
    per = heads // 2
    step = 2 * HD * per + NOTE_ROWS
    side = lax.rem(lax.axis_index("mp"), 2)

    def exchange(x, bits, far=0, back=False):
        pairs = []
        for i in range(n_blk):
            square, pair, lane = i // 4, i // 2 % 2, i % 2
            for m in range(n_mp):
                other, core = m // 2, m % 2
                blk = (square ^ far) * 4 + (pair ^ bits) * 2 + 1 - core
                link = (i * n_mp + m, blk * n_mp + other * 2 + lane)
                pairs.append(link[::-1] if back else link)
        return lax.ppermute(x, ("blk", "mp"), pairs)

    def across(x, bit):
        return lax.ppermute(x, "blk", [(i, i ^ bit) for i in range(n_blk)])

    def across_mp(x, bit):
        return lax.ppermute(x, "mp", [(i, i ^ bit) for i in range(n_mp)])

    group = jnp.where(block_live == 1, block_slot * GROUPS // n_blk, -1).astype(bf16)
    tag = jnp.broadcast_to(group, (NOTE_ROWS, HD))
    early = call(
        functools.partial(pack_kernel, per),
        [((step, HD), bf16)] * (3 if n_blk == 8 else 1),
        (HBM, HBM, VMEM),
        [pltpu.SemaphoreType.DMA(((6 if n_blk == 8 else 2) * per,))],
    )(prefix_keys, prefix_values, tag)
    near = exchange(early[0], 1)
    fars = [exchange(early[1 + k], k, far=1) for k in (0, 1)] if n_blk == 8 else []
    normed, query, *packs = call(
        functools.partial(query_kernel, per),
        [((rows, width), bf16), ((rows, local_width), bf16)]
        + [((per * rows + n, HD), bf16) for n in (step, NOTE_ROWS)],
        (HBM, HBM, VMEM) + (HBM,) * 6,
        [
            pltpu.VMEM((rows, width), bf16),
            pltpu.VMEM(w_query.shape, bf16),
            pltpu.VMEM((1, width), f32),
            pltpu.VMEM((1, width), f32),
            pltpu.VMEM(segment.shape, i32),
            pltpu.SMEM(request_group.shape, i32),
            pltpu.SemaphoreType.DMA((4 + ROW_CUTS + W_CUTS + 2 * per,)),
        ],
        cost=Q,
    )(
        prefix_keys,
        prefix_values,
        tag,
        hidden_in,
        w_query,
        norm_gain.reshape(1, width),
        norm_bias.reshape(1, width),
        segment,
        request_group,
    )
    asks = {k: exchange(packs[k], k) for k in ORDER[::-1]}
    asks = [asks[k] for k in ORDER]
    suffix_sum, suffix_log = call(
        functools.partial(suffix_kernel, heads),
        [((local_width, rows), f32), ((max(heads, 8), rows), f32)],
        (VMEM,) * 2 + (HBM,) * 3,
        [
            pltpu.VMEM(segment.shape, i32),
            pltpu.VMEM(w_key.shape, bf16),
            pltpu.VMEM(w_value.shape, bf16),
            pltpu.SemaphoreType.DMA((1 + 2 * W_CUTS,)),
        ],
        cost=SFX,
    )(normed, query, segment, w_key, w_value)
    last = asks[1][per * rows :]
    if fars:
        join = call(join_kernel, [((2 * step, HD), bf16)], (VMEM,) * 3, cost=JOIN1)
        first = join(suffix_log, fars[0], near)[0]
        first_other = across_mp(first, 1)
        wait = call(gate_kernel, [((8, HD), f32)], (VMEM,) * 2, cost=JOIN)
        gate = wait(first, fars[1])[0]
        second = call(last_join_kernel, [((2 * step, HD), bf16)], (VMEM,) * 3)(gate, fars[1], asks[1])[0]
        blocks = [first, first_other, second]
        others = [across_mp(second, 1)]
    else:
        blocks = [near, across_mp(near, 1)]
        others, bit = [across_mp(last, 1)], 4
        while bit < n_blk:
            others = others + [across(jnp.concatenate(blocks + [last] + others, axis=0), bit)]
            bit *= 2
    state, summed = call(
        functools.partial(first_kernel, rows, per),
        [((8, heads * rows), f32), ((HD, heads * rows), f32)],
        (VMEM,) * (2 + len(blocks)),
        cost=30,
    )(*asks[::-1], *blocks)
    backs = call(
        functools.partial(second_kernel, rows, per),
        [((per * HD + NOTE_ROWS, rows), bf16)] * 2,
        (VMEM,) * (4 + len(others)),
    )(*asks[::-1], state, summed, *others)
    backs = dict(zip(ORDER, backs))
    backs = [exchange(backs[k], k, back=True) for k in BACK]

    keep, send = call(
        functools.partial(project_kernel, per),
        [((rows // 2, width), f32), ((rows // 2, width), bf16)],
        (VMEM,) * 5,
        [pltpu.VMEM((local_width, rows), bf16), pltpu.VMEM((rows, width), f32)],
    )(suffix_sum, suffix_log, w_out, *backs)

    mine = (keep + across_mp(send, 1).astype(f32)).astype(bf16)
    bit = 2
    while bit < n_mp:
        mine = (mine.astype(f32) + across_mp(mine, bit).astype(f32)).astype(bf16 if 2 * bit < n_mp else f32)
        bit *= 2
    inputs = lax.dynamic_slice_in_dim(hidden_in, side * (rows // 2), rows // 2, 0)
    done = (inputs.astype(f32) + mine.astype(f32)).astype(bf16)
    other = across_mp(done, 1)
    whole = call(
        own_half_kernel,
        [((rows, width), bf16)],
        (VMEM,),
        [pltpu.SemaphoreType.DMA((1,))],
        (HBM,),
    )(done)[0]
    return call(
        other_half_kernel,
        [((rows, width), bf16)],
        (VMEM, HBM),
        [pltpu.SemaphoreType.DMA((1,))],
        (HBM,),
        {1: 0},
    )(other, whole)[0]


def solution(mesh):
    return jax.shard_map(
        local,
        mesh=mesh,
        in_specs=(
            P("blk", None),
            P(),
            P(),
            P(None, "mp"),
            P(None, "mp"),
            P(None, "mp"),
            P("mp", None),
            P("blk", None, "mp"),
            P("blk", None, "mp"),
            P("blk", None),
            P("blk", None),
            P("blk"),
            P("blk"),
        ),
        out_specs=P("blk", None),
        check_vma=False,
    )
```
